512 devices in a mesh: dp: 64 (over z, y_hi, core), feat: 8 (over y_lo, x).
Axes of the slice: x: 4, y: 8 (y_hi: 4, y_lo: 2; y = y_hi * 2 + y_lo), z: 8, core: 2. Of those that a mesh axis runs over, the one named last changes fastest.
Arguments:
- views: float32 [8192, 1536], P('dp', 'feat'), may hold values from -0.2 to 0.2
- partner: int32 [8192], P('dp'), may hold values from 0 to 8191, as said below
Outputs:
- loss: float32 [], replicated
- grad_views: float32 [8192, 1536], P('dp', 'feat')
The draws below stay inside these ranges and needn't reach their ends.
Inputs may be any that keep to these rules, and one draw needn't show every extreme that they name: partner pairs the views: partner[partner[i]] == i and partner[i] != i.
All inputs are finite; a program needn't handle non-finite values.
Results may differ from the reference program's by a relative error of at most 0.0003.
Values sent between devices are 32-bit elements; how exact they have to be, the bound alone decides.
No kernel may reach another device: no remote copies, remote signals or barrier semaphores. Data moves between devices by JAX's collectives and lax.ppermute only.
A program may use at most 64 MiB of HBM per device.

```python
import jax
import jax.numpy as jnp
from jax import lax

E = 1536
ROWS_DEV = 128
N = 8192
N_DP = 64


def draw_partner(key, part):
    key = jax.random.fold_in(key, 5)
    order = jax.random.permutation(key, N).astype(jnp.int32)
    firsts = order[0::2]
    seconds = order[1::2]
    result = jnp.zeros((N,), jnp.int32)
    result = result.at[firsts].set(seconds)
    result = result.at[seconds].set(firsts)
    return result


def levels(key, shape, cuts, smallest, largest):
    def one(dim, parts):
        heights = jax.random.uniform(jax.random.fold_in(jax.random.fold_in(key, 6), dim), (parts,), jnp.float32, smallest / len(cuts), largest / len(cuts))
        return jnp.repeat(jnp.exp(heights), shape[dim] // parts).reshape((-1,) + (1,) * (len(shape) - dim - 1))

    gain = one(*cuts[0])
    for cut in cuts[1:]:
        gain = gain * one(*cut)
    return gain


def centred(rng, dims, deviation, bound, shards=(), held_as=jnp.bfloat16):
    drawn = jax.random.normal(rng, dims, jnp.float32) * deviation
    if len(shards) > 0:
        drawn = levels(rng, dims, shards, -0.22, 0.18) * drawn
    return jnp.clip(drawn, min=-bound, max=bound).astype(held_as)


def setup_inputs(seed: int = 0) -> dict:
    keys = jax.random.split(jax.random.key(seed), 3)
    views = centred(keys[0], (N, E), 0.03, 0.2, ((0, 64), (1, 8)), jnp.float32)
    partner = draw_partner(jax.random.fold_in(keys[2], 71), 0)
    return dict(views=views, partner=partner)


def reference(views, partner):
    inv_tau = 10.0
    norms_sq = lax.optimization_barrier(jnp.sum(views * views, axis=1))
    scale = lax.rsqrt(norms_sq + 1e-06)
    units = views * scale[:, None]
    cols = jnp.arange(N, dtype=jnp.int32)
    blocks = units.reshape(N_DP, ROWS_DEV, E)
    pblocks = partner.reshape(N_DP, ROWS_DEV)
    starts = jnp.arange(N_DP, dtype=jnp.int32) * ROWS_DEV

    def block_scores(block, start):
        scores = jnp.dot(block, units.T, precision=lax.Precision.HIGHEST) * inv_tau
        rows = start + jnp.arange(ROWS_DEV, dtype=jnp.int32)
        diag = cols[None, :] == rows[:, None]
        return (scores, diag)

    def first(item):
        block, start, part = item
        scores, diag = block_scores(block, start)
        lse = jnp.log(lax.optimization_barrier(jnp.sum(jnp.where(diag, 0.0, jnp.exp(scores)), axis=1)))
        pos = lax.optimization_barrier(jnp.sum(jnp.where(cols[None, :] == part[:, None], scores, 0.0), axis=1))
        return (lse, lse - pos)
    lse_blocks, row_loss = lax.map(first, (blocks, starts, pblocks))
    lse_all = lse_blocks.reshape(N)

    def second(item):
        block, start, part, lse = item
        scores, diag = block_scores(block, start)
        both = jnp.exp(scores - lse[:, None]) + jnp.exp(scores - lse_all[None, :])
        weights = jnp.where(diag, 0.0, both) - 2.0 * (cols[None, :] == part[:, None]).astype(jnp.float32)
        return jnp.dot(weights, units, precision=lax.Precision.HIGHEST) * inv_tau
    grad_units = lax.map(second, (blocks, starts, pblocks, lse_blocks)).reshape(N, E)
    proj = lax.optimization_barrier(jnp.sum(units * grad_units, axis=1))
    grad_views = (grad_units - units * proj[:, None]) * scale[:, None]
    loss = jnp.sum(row_loss) / N
    return (loss, grad_views)
```

```python
import jax
import jax.numpy as jnp
from jax import lax
from jax.experimental import pallas as pl
from jax.experimental.pallas import tpu as pltpu
from jax.sharding import Mesh, PartitionSpec as P

NZ, NYH, NC, NYL, NX = 8, 4, 2, 2, 4
NF = NYL * NX
ROWS = 128
FEAT = 192
WIDE = NF * FEAT
CHUNK = ROWS // NF
NCOL = NZ * NYH * CHUNK
PIECE = FEAT + 8
TOTAL = 8192
INV_TAU = 10.0
VMEM = pl.BlockSpec(memory_space=pltpu.VMEM)
SMEM = pl.BlockSpec(memory_space=pltpu.SMEM)
PARAMS = pltpu.CompilerParams(vmem_limit_bytes=48 * 1024 * 1024)


def f32(*shape):
    return jax.ShapeDtypeStruct(shape, jnp.float32)


def split(x):
    hi = x.astype(jnp.bfloat16)
    lo = (x - hi.astype(jnp.float32)).astype(jnp.bfloat16)
    return hi, lo


def dot3(a, b, dims):
    def one(x, y):
        return lax.dot_general(x, y, (dims, ((), ())), preferred_element_type=jnp.float32)
    return one(a[0], b[0]) + (one(a[0], b[1]) + one(a[1], b[0]))


def column(x):
    return jnp.broadcast_to(x, (ROWS, ROWS)).T[:, :1]


def pack(x):
    half = CHUNK // 2
    return jnp.concatenate([x[:, :ROWS], jnp.concatenate([x[:half, ROWS:], x[half:, ROWS:]], axis=1)], axis=0)


def unpack(x):
    tail = x[CHUNK:, :]
    rest = FEAT - ROWS
    return jnp.concatenate([x[:CHUNK, :], jnp.concatenate([tail[:, :rest], tail[:, rest:]], axis=0)], axis=1)


def chunk_kernel(view_ref, out_ref):
    x = view_ref[...].T
    for f in range(NF):
        piece = pack(x[f * CHUNK:(f + 1) * CHUNK, :])
        for y in range(NYH):
            out_ref[y * NF + f] = piece


def column_kernel(piece_ref, view_ref, unit_ref, copies_ref):
    for y in range(NYH):
        x = jnp.concatenate([unpack(piece_ref[y * NF + f]) for f in range(NF)], axis=1)
        scale = lax.rsqrt(jnp.sum(x * x, axis=1, keepdims=True) + 1e-06)
        unit_ref[y * CHUNK:(y + 1) * CHUNK, :] = x * scale
    for f in range(NF):
        copies_ref[f] = view_ref[...]


def norm_kernel(piece_ref, unit_ref, scale_ref):
    x = piece_ref[...].reshape(WIDE, ROWS)
    scale = lax.rsqrt(jnp.sum(x * x, axis=0, keepdims=True) + 1e-06)
    scale_ref[...] = scale
    unit_ref[...] = (x * scale).T


def tile_masks(pos_ref, half, part):
    zy, core, me = pos_ref[0], pos_ref[1], pos_ref[2]
    lane = lax.broadcasted_iota(jnp.int32, (1, NCOL), 1)
    col = ((lane // CHUNK) * NC + core) * ROWS + me * CHUNK + lane % CHUNK
    row = (zy * NC + half) * ROWS + lax.broadcasted_iota(jnp.int32, (ROWS, 1), 0)
    return col == row, col == part


def score_kernel(pos_ref, own_ref, oth_ref, cols_ref, ownp_ref, othp_ref, s_ref, row_ref, col_ref, hi, lo):
    core = pos_ref[1]
    for j, ref in enumerate((own_ref, oth_ref)):
        hi[j], lo[j] = split(ref[...])
    rows = (hi[...].reshape(NC * ROWS, WIDE), lo[...].reshape(NC * ROWS, WIDE))
    step = 256
    for c in range(0, NCOL, step):
        s_ref[:, c:c + step] = INV_TAU * dot3(rows, split(cols_ref[c:c + step, :]), ((1,), (1,)))
    colsum = jnp.zeros((1, NCOL), jnp.float32)
    pos = jnp.zeros((1, ROWS), jnp.float32)
    sums = []
    for j, part in enumerate((ownp_ref, othp_ref)):
        s = s_ref[j * ROWS:(j + 1) * ROWS, :]
        diag, hit = tile_masks(pos_ref, core ^ j, part[...])
        e = jnp.where(diag, 0.0, jnp.exp(s))
        colsum = colsum + jnp.sum(e, axis=0, keepdims=True)
        lanes = e[:, :ROWS]
        hits = jnp.sum(jnp.where(hit, s, 0.0), axis=0, keepdims=True)
        for c in range(NCOL // ROWS):
            pos = pos + hits[:, c * ROWS:(c + 1) * ROWS]
            if c:
                lanes = lanes + e[:, c * ROWS:(c + 1) * ROWS]
        sums.append(jnp.sum(lanes.T, axis=0, keepdims=True))
    first = core == 0
    row = jnp.concatenate([jnp.where(first, sums[0], sums[1]), jnp.where(first, sums[1], sums[0]),
                           jnp.zeros((8 - NC, ROWS), jnp.float32)], axis=0)
    nrow = NCOL // ROWS
    col = jnp.concatenate([colsum[:, c * ROWS:(c + 1) * ROWS] for c in range(nrow)]
                          + [pos, jnp.zeros((7 - nrow, ROWS), jnp.float32)], axis=0)
    for k in range(NC * NF):
        row_ref[k] = row
    for k in range(NZ * NYH):
        col_ref[k] = col


def grad_kernel(pos_ref, s_ref, own_ref, oth_ref, cols_ref, ownp_ref, othp_ref, rows_ref, cols_l_ref, mine_ref, theirs_ref, w_hi, w_lo):
    core = pos_ref[1]
    row_l = jnp.sum(rows_ref[...], axis=0)
    col_l = jnp.sum(cols_l_ref[...], axis=0)
    nrow = NCOL // ROWS
    col_inv = jnp.concatenate([1.0 / col_l[c:c + 1, :] for c in range(nrow)], axis=1)
    loss = jnp.sum(jnp.log(col_l[:nrow, :]), axis=0, keepdims=True) - col_l[nrow:nrow + 1, :]
    projs = []
    for j, part in enumerate((ownp_ref, othp_ref)):
        s = s_ref[j * ROWS:(j + 1) * ROWS, :]
        half = core ^ j
        diag, hit = tile_masks(pos_ref, half, part[...])
        inv = column(1.0 / jnp.where(half == 0, row_l[0:1, :], row_l[1:2, :]))
        w = jnp.where(diag, 0.0, jnp.exp(s) * (inv + col_inv)) - jnp.where(hit, 2.0, 0.0)
        projs.append(jnp.sum(w * s, axis=1, keepdims=True))
        w_hi[j], w_lo[j] = split(w)
    weights = (w_hi[...].reshape(NC * ROWS, NCOL), w_lo[...].reshape(NC * ROWS, NCOL))
    step = 2 * FEAT
    tail = jnp.concatenate([loss, jnp.zeros((7, ROWS), jnp.float32)], axis=0)
    for c in range(WIDE // step):
        at = slice(c * step, (c + 1) * step)
        g = INV_TAU * dot3(weights, split(cols_ref[:, at]), ((1,), (0,)))
        for j, (units, out) in enumerate(((own_ref, mine_ref), (oth_ref, theirs_ref))):
            t = (g[j * ROWS:(j + 1) * ROWS, :] - units[:, at] * projs[j]).T
            for p in range(2):
                out[2 * c + p, :FEAT, :] = t[p * FEAT:(p + 1) * FEAT, :]
                out[2 * c + p, FEAT:, :] = tail


def last_kernel(piece_ref, scale_ref, loss_ref, grad_ref):
    total = jnp.sum(piece_ref[...], axis=0)
    loss_ref[...] = jnp.sum(total[FEAT:FEAT + 1, :], axis=1, keepdims=True) / TOTAL
    grad_ref[...] = total[:FEAT, :] * scale_ref[...]


def swap(x, axes, size, k):
    return lax.ppermute(x, axes, [(i, i ^ k) for i in range(size)])


def trade(x, axes):
    return lax.all_to_all(x, axes, 0, 0, tiled=True)


def call(body, name, outs, args, scratch=()):
    return pl.pallas_call(
        body,
        out_shape=outs,
        in_specs=[SMEM if a.shape == (3,) else VMEM for a in args],
        out_specs=[VMEM] * len(outs),
        scratch_shapes=list(scratch),
        compiler_params=PARAMS,
        name=name,
    )(*args)


def per_device(views, partner):
    zy = lax.axis_index(("z", "yh"))
    core = lax.axis_index("core")
    me = lax.axis_index(("yl", "x"))
    pos = jnp.stack([zy, core, me]).astype(jnp.int32)
    feat = ("yl", "x")

    own_p = partner.reshape(ROWS, 1)
    oth_p = swap(partner, "core", NC, 1).reshape(ROWS, 1)
    packed = CHUNK * FEAT // ROWS
    chunks, = call(chunk_kernel, "chunks", [f32(NYH * NF, packed, ROWS)], [views.T])
    chunks = trade(chunks, ("yh", "yl", "x"))
    chunk, copies = call(column_kernel, "columns", [f32(NYH * CHUNK, WIDE), f32(NF, FEAT, ROWS)], [chunks, views.T])
    cols = lax.all_gather(chunk, "z", axis=0, tiled=True)
    own, scale = call(norm_kernel, "norm", [f32(ROWS, WIDE), f32(1, ROWS)], [trade(copies, feat)])
    oth = swap(own, "core", NC, 1)
    s, row, col = call(
        score_kernel, "scores",
        [f32(NC * ROWS, NCOL), f32(NC * NF, 8, ROWS), f32(NZ * NYH, 8, ROWS)],
        [pos, own, oth, cols, own_p, oth_p],
        [pltpu.VMEM((NC, ROWS, WIDE), jnp.bfloat16)] * 2,
    )
    rows_l = trade(row, ("core", "yl", "x"))
    cols_l = trade(col, ("z", "yh"))
    mine, theirs = call(
        grad_kernel, "gradient",
        [f32(NF, PIECE, ROWS)] * 2,
        [pos, s, own, oth, cols, own_p, oth_p, rows_l, cols_l],
        [pltpu.VMEM((NC, ROWS, NCOL), jnp.bfloat16)] * 2,
    )
    pieces = trade(mine + swap(theirs, "core", NC, 1), feat)
    loss, grad = call(last_kernel, "finish", [f32(1, 1), f32(FEAT, ROWS)], [pieces, scale])
    return loss.reshape(()), grad.T


def solution(mesh):
    fine = Mesh(mesh.devices.reshape(NZ, NYH, NC, NYL, NX), ("z", "yh", "core", "yl", "x"))
    rows = ("z", "yh", "core")
    return jax.shard_map(
        per_device,
        mesh=fine,
        in_specs=(P(rows, ("yl", "x")), P(rows)),
        out_specs=(P(), P(rows, ("yl", "x"))),
        check_vma=False,
    )
```

```python
import jax
import jax.numpy as jnp
from jax import lax
from jax.experimental import pallas as pl
from jax.experimental.pallas import tpu as pltpu
from jax.sharding import Mesh, PartitionSpec as P

NZ, NYH, NC, NYL, NX = 8, 4, 2, 2, 4
NF = NYL * NX
ROWS = 128
FEAT = 192
WIDE = NF * FEAT
CHUNK = ROWS // NF
NCOL = NZ * NYH * CHUNK
PIECE = FEAT + 8
PACKED = CHUNK * FEAT // ROWS
TOTAL = 8192
INV_TAU = 10.0
VMEM = pl.BlockSpec(memory_space=pltpu.VMEM)
SMEM = pl.BlockSpec(memory_space=pltpu.SMEM)
HBM = pl.BlockSpec(memory_space=pltpu.HBM)
PARAMS = pltpu.CompilerParams(vmem_limit_bytes=20 * 1024 * 1024)


def f32(*shape):
    return jax.ShapeDtypeStruct(shape, jnp.float32)


def split(x):
    hi = x.astype(jnp.bfloat16)
    lo = (x - hi.astype(jnp.float32)).astype(jnp.bfloat16)
    return hi, lo


def dot3(a, b, dims):
    def one(x, y):
        return lax.dot_general(x, y, (dims, ((), ())), preferred_element_type=jnp.float32)
    return one(a[0], b[0]) + (one(a[0], b[1]) + one(a[1], b[0]))


def column(x):
    return jnp.broadcast_to(x, (ROWS, ROWS)).T[:, :1]


def pack(x):
    half = CHUNK // 2
    return jnp.concatenate([x[:, :ROWS], jnp.concatenate([x[:half, ROWS:], x[half:, ROWS:]], axis=1)], axis=0)


def unpack(x):
    tail = x[CHUNK:, :]
    rest = FEAT - ROWS
    return jnp.concatenate([x[:CHUNK, :], jnp.concatenate([tail[:, :rest], tail[:, rest:]], axis=0)], axis=1)


def chunk_kernel(view_ref, out_ref):
    x = view_ref[...].T
    for f in range(NF):
        low, across = f // NX, f % NX
        out_ref[across, low * PACKED:(low + 1) * PACKED, :] = pack(x[f * CHUNK:(f + 1) * CHUNK, :])


def half_kernel(piece_ref, out_ref):
    for low in range(NYL):
        at = slice(low * PACKED, (low + 1) * PACKED)
        x = jnp.concatenate([unpack(piece_ref[k, at, :]) for k in range(NX)], axis=1)
        for y in range(NYH):
            out_ref[y * NYL + low] = x


def column_kernel(piece_ref, view_ref, unit_ref, copies_ref):
    for y in range(NYH):
        x = jnp.concatenate([piece_ref[y * NYL + low] for low in range(NYL)], axis=1)
        scale = lax.rsqrt(jnp.sum(x * x, axis=1, keepdims=True) + 1e-06)
        unit_ref[y * CHUNK:(y + 1) * CHUNK, :] = x * scale
    for f in range(NF):
        copies_ref[f] = view_ref[...]


def norm_kernel(piece_ref, unit_ref, scale_ref):
    x = piece_ref[...].reshape(WIDE, ROWS)
    scale = lax.rsqrt(jnp.sum(x * x, axis=0, keepdims=True) + 1e-06)
    scale_ref[...] = scale
    unit_ref[...] = (x * scale).T


def tile_masks(pos_ref, half, part):
    zy, core, me = pos_ref[0], pos_ref[1], pos_ref[2]
    lane = lax.broadcasted_iota(jnp.int32, (1, NCOL), 1)
    col = ((lane // CHUNK) * NC + core) * ROWS + me * CHUNK + lane % CHUNK
    row = (zy * NC + half) * ROWS + lax.broadcasted_iota(jnp.int32, (ROWS, 1), 0)
    return col == row, col == part


def score_kernel(pos_ref, own_ref, oth_ref, cols_hbm, ownp_ref, othp_ref, s_ref, row_ref, col_ref, chi_ref, clo_ref, hi, lo, cols, sems):
    core = pos_ref[1]
    step = 256
    copies = []
    for i in range(NCOL // step):
        at = pl.ds(i * step, step)
        copies.append(pltpu.make_async_copy(cols_hbm.at[at, :], cols.at[at, :], sems.at[i]))
        copies[-1].start()
    for j, ref in enumerate((own_ref, oth_ref)):
        hi[j], lo[j] = split(ref[...])
    rows = (hi[...].reshape(NC * ROWS, WIDE), lo[...].reshape(NC * ROWS, WIDE))
    for i, copy in enumerate(copies):
        at = slice(i * step, (i + 1) * step)
        copy.wait()
        h, l = split(cols[at, :])
        chi_ref[at, :] = h
        clo_ref[at, :] = l
        s_ref[:, at] = INV_TAU * dot3(rows, (h, l), ((1,), (1,)))
    colsum = jnp.zeros((1, NCOL), jnp.float32)
    pos = jnp.zeros((1, ROWS), jnp.float32)
    sums = []
    for j, part in enumerate((ownp_ref, othp_ref)):
        s = s_ref[j * ROWS:(j + 1) * ROWS, :]
        diag, hit = tile_masks(pos_ref, core ^ j, part[...])
        e = jnp.where(diag, 0.0, jnp.exp(s))
        colsum = colsum + jnp.sum(e, axis=0, keepdims=True)
        lanes = e[:, :ROWS]
        hits = jnp.sum(jnp.where(hit, s, 0.0), axis=0, keepdims=True)
        for c in range(NCOL // ROWS):
            pos = pos + hits[:, c * ROWS:(c + 1) * ROWS]
            if c:
                lanes = lanes + e[:, c * ROWS:(c + 1) * ROWS]
        sums.append(jnp.sum(lanes.T, axis=0, keepdims=True))
    first = core == 0
    row = jnp.concatenate([jnp.where(first, sums[0], sums[1]), jnp.where(first, sums[1], sums[0]),
                           jnp.zeros((8 - NC, ROWS), jnp.float32)], axis=0)
    nrow = NCOL // ROWS
    col = jnp.concatenate([colsum[:, c * ROWS:(c + 1) * ROWS] for c in range(nrow)]
                          + [pos, jnp.zeros((7 - nrow, ROWS), jnp.float32)], axis=0)
    for k in range(NC * NYL):
        row_ref[k] = row
    for k in range(NYH):
        col_ref[k] = col


def relay_kernel(rows_ref, cols_ref, row_ref, col_ref):
    row = jnp.sum(rows_ref[...], axis=0)
    col = jnp.sum(cols_ref[...], axis=0)
    for k in range(NX):
        row_ref[k] = row
    for k in range(NZ):
        col_ref[k] = col


def grad_kernel(pos_ref, s_ref, own_ref, oth_ref, chi_ref, clo_ref, ownp_ref, othp_ref, rows_ref, cols_l_ref, mine_ref, theirs_ref, w_hi, w_lo):
    core = pos_ref[1]
    row_l = jnp.sum(rows_ref[...], axis=0)
    col_l = jnp.sum(cols_l_ref[...], axis=0)
    nrow = NCOL // ROWS
    col_inv = jnp.concatenate([1.0 / col_l[c:c + 1, :] for c in range(nrow)], axis=1)
    loss = jnp.sum(jnp.log(col_l[:nrow, :]), axis=0, keepdims=True) - col_l[nrow:nrow + 1, :]
    projs = []
    for j, part in enumerate((ownp_ref, othp_ref)):
        s = s_ref[j * ROWS:(j + 1) * ROWS, :]
        half = core ^ j
        diag, hit = tile_masks(pos_ref, half, part[...])
        inv = column(1.0 / jnp.where(half == 0, row_l[0:1, :], row_l[1:2, :]))
        w = jnp.where(diag, 0.0, jnp.exp(s) * (inv + col_inv)) - jnp.where(hit, 2.0, 0.0)
        projs.append(jnp.sum(w * s, axis=1, keepdims=True))
        w_hi[j], w_lo[j] = split(w)
    weights = (w_hi[...].reshape(NC * ROWS, NCOL), w_lo[...].reshape(NC * ROWS, NCOL))
    step = 2 * FEAT
    tail = jnp.concatenate([loss, jnp.zeros((7, ROWS), jnp.float32)], axis=0)
    for c in range(WIDE // step):
        at = slice(c * step, (c + 1) * step)
        g = INV_TAU * dot3(weights, (chi_ref[:, at], clo_ref[:, at]), ((1,), (0,)))
        for j, (units, out) in enumerate(((own_ref, mine_ref), (oth_ref, theirs_ref))):
            t = (g[j * ROWS:(j + 1) * ROWS, :] - units[:, at] * projs[j]).T
            for p in range(2):
                out[2 * c + p, :FEAT, :] = t[p * FEAT:(p + 1) * FEAT, :]
                out[2 * c + p, FEAT:, :] = tail


def last_kernel(piece_ref, scale_ref, loss_ref, grad_ref):
    total = jnp.sum(piece_ref[...], axis=0)
    loss_ref[...] = jnp.sum(total[FEAT:FEAT + 1, :], axis=1, keepdims=True) / TOTAL
    grad_ref[...] = total[:FEAT, :] * scale_ref[...]


def swap(x, axes, size, k):
    return lax.ppermute(x, axes, [(i, i ^ k) for i in range(size)])


def trade(x, axes):
    return lax.all_to_all(x, axes, 0, 0, tiled=True)


def call(body, name, outs, args, scratch=(), far=()):
    return pl.pallas_call(
        body,
        out_shape=outs,
        in_specs=[SMEM if a.shape == (3,) else HBM if i in far else VMEM for i, a in enumerate(args)],
        out_specs=[VMEM] * len(outs),
        scratch_shapes=list(scratch),
        compiler_params=PARAMS,
        name=name,
    )(*args)


def per_device(views, partner):
    zy = lax.axis_index(("z", "yh"))
    core = lax.axis_index("core")
    me = lax.axis_index(("yl", "x"))
    pos = jnp.stack([zy, core, me]).astype(jnp.int32)
    feat = ("yl", "x")

    own_p = partner.reshape(ROWS, 1)
    oth_p = swap(partner, "core", NC, 1).reshape(ROWS, 1)
    chunks, = call(chunk_kernel, "chunks", [f32(NX, NYL * PACKED, ROWS)], [views.T])
    halves, = call(half_kernel, "halves", [f32(NYH * NYL, CHUNK, WIDE // NYL)], [trade(chunks, "x")])
    chunk, copies = call(column_kernel, "columns", [f32(NYH * CHUNK, WIDE), f32(NF, FEAT, ROWS)],
                         [trade(halves, ("yh", "yl")), views.T])
    cols = lax.all_gather(chunk, "z", axis=0, tiled=True)
    own, scale = call(norm_kernel, "norm", [f32(ROWS, WIDE), f32(1, ROWS)], [trade(copies, feat)])
    oth = swap(own, "core", NC, 1)
    bf16 = jax.ShapeDtypeStruct((NCOL, WIDE), jnp.bfloat16)
    s, row, col, chi, clo = call(
        score_kernel, "scores",
        [f32(NC * ROWS, NCOL), f32(NC * NYL, 8, ROWS), f32(NYH, 8, ROWS), bf16, bf16],
        [pos, own, oth, cols, own_p, oth_p],
        [pltpu.VMEM((NC, ROWS, WIDE), jnp.bfloat16)] * 2
        + [pltpu.VMEM((NCOL, WIDE), jnp.float32), pltpu.SemaphoreType.DMA((NCOL // 256,))],
        far=(3,),
    )
    row, col = call(relay_kernel, "relay", [f32(NX, 8, ROWS), f32(NZ, 8, ROWS)],
                    [trade(row, ("core", "yl")), trade(col, "yh")])
    mine, theirs = call(
        grad_kernel, "gradient",
        [f32(NF, PIECE, ROWS)] * 2,
        [pos, s, own, oth, chi, clo, own_p, oth_p, trade(row, "x"), trade(col, "z")],
        [pltpu.VMEM((NC, ROWS, NCOL), jnp.bfloat16)] * 2,
    )
    pieces = trade(mine + swap(theirs, "core", NC, 1), feat)
    loss, grad = call(last_kernel, "finish", [f32(1, 1), f32(FEAT, ROWS)], [pieces, scale])
    return loss.reshape(()), grad.T


def solution(mesh):
    fine = Mesh(mesh.devices.reshape(NZ, NYH, NC, NYL, NX), ("z", "yh", "core", "yl", "x"))
    rows = ("z", "yh", "core")
    return jax.shard_map(
        per_device,
        mesh=fine,
        in_specs=(P(rows, ("yl", "x")), P(rows)),
        out_specs=(P(), P(rows, ("yl", "x"))),
        check_vma=False,
    )
```

```python
import jax
import jax.numpy as jnp
from jax import lax
from jax.experimental import pallas as pl
from jax.experimental.pallas import tpu as pltpu
from jax.sharding import Mesh, PartitionSpec as P

NZ, NYH, NC, NYL, NX = 8, 4, 2, 2, 4
NF = NYL * NX
ROWS = 128
FEAT = 192
WIDE = NF * FEAT
CHUNK = ROWS // NF
NCOL = NZ * NYH * CHUNK
PIECE = FEAT + 8
TOTAL = 8192
INV_TAU = 10.0
VMEM = pl.BlockSpec(memory_space=pltpu.VMEM)
SMEM = pl.BlockSpec(memory_space=pltpu.SMEM)
HBM = pl.BlockSpec(memory_space=pltpu.HBM)
MIB = 1024 * 1024


def f32(*shape):
    return jax.ShapeDtypeStruct(shape, jnp.float32)


def split(x):
    hi = x.astype(jnp.bfloat16)
    lo = (x - hi.astype(jnp.float32)).astype(jnp.bfloat16)
    return hi, lo


def dot3(a, b, dims):
    def one(x, y):
        return lax.dot_general(x, y, (dims, ((), ())), preferred_element_type=jnp.float32)
    return one(a[0], b[0]) + (one(a[0], b[1]) + one(a[1], b[0]))


def column(x):
    return jnp.broadcast_to(x, (ROWS, ROWS)).T[:, :1]


def pack(x):
    half = CHUNK // 2
    return jnp.concatenate([x[:, :ROWS], jnp.concatenate([x[:half, ROWS:], x[half:, ROWS:]], axis=1)], axis=0)


def unpack(x):
    tail = x[CHUNK:, :]
    rest = FEAT - ROWS
    return jnp.concatenate([x[:CHUNK, :], jnp.concatenate([tail[:, :rest], tail[:, rest:]], axis=0)], axis=1)


def chunk_kernel(view_ref, out_ref):
    x = view_ref[...].T
    for f in range(NF):
        piece = pack(x[f * CHUNK:(f + 1) * CHUNK, :])
        for y in range(NYH):
            out_ref[y * NF + f] = piece


def column_kernel(piece_ref, unit_ref):
    for y in range(NYH):
        x = jnp.concatenate([unpack(piece_ref[y * NF + f]) for f in range(NF)], axis=1)
        scale = lax.rsqrt(jnp.sum(x * x, axis=1, keepdims=True) + 1e-06)
        unit_ref[y * CHUNK:(y + 1) * CHUNK, :] = x * scale


def norm_kernel(piece_ref, unit_ref, scale_ref):
    x = piece_ref[...]
    scale = lax.rsqrt(jnp.sum(x * x, axis=0, keepdims=True) + 1e-06)
    scale_ref[...] = scale
    unit_ref[...] = (x * scale).T


def tile_masks(pos_ref, half, part):
    zy, core, me = pos_ref[0], pos_ref[1], pos_ref[2]
    lane = lax.broadcasted_iota(jnp.int32, (1, NCOL), 1)
    col = ((lane // CHUNK) * NC + core) * ROWS + me * CHUNK + lane % CHUNK
    row = (zy * NC + half) * ROWS + lax.broadcasted_iota(jnp.int32, (ROWS, 1), 0)
    return col == row, col == part


def score_kernel(pos_ref, own_ref, oth_ref, cols_hbm, ownp_ref, othp_ref, s_ref, row_ref, col_ref, hi, lo, cols, sems):
    core = pos_ref[1]
    step = 256
    copies = []
    for i in range(NCOL // step):
        at = pl.ds(i * step, step)
        copies.append(pltpu.make_async_copy(cols_hbm.at[at, :], cols.at[at, :], sems.at[i]))
        copies[-1].start()
    for j, ref in enumerate((own_ref, oth_ref)):
        hi[j], lo[j] = split(ref[...])
    rows = (hi[...].reshape(NC * ROWS, WIDE), lo[...].reshape(NC * ROWS, WIDE))
    for i, copy in enumerate(copies):
        at = slice(i * step, (i + 1) * step)
        copy.wait()
        s_ref[:, at] = INV_TAU * dot3(rows, split(cols[at, :]), ((1,), (1,)))
    colsum = jnp.zeros((1, NCOL), jnp.float32)
    pos = jnp.zeros((1, ROWS), jnp.float32)
    sums = []
    for j, part in enumerate((ownp_ref, othp_ref)):
        s = s_ref[j * ROWS:(j + 1) * ROWS, :]
        diag, hit = tile_masks(pos_ref, core ^ j, part[...])
        e = jnp.where(diag, 0.0, jnp.exp(s))
        colsum = colsum + jnp.sum(e, axis=0, keepdims=True)
        lanes = e[:, :ROWS]
        hits = jnp.sum(jnp.where(hit, s, 0.0), axis=0, keepdims=True)
        for c in range(NCOL // ROWS):
            pos = pos + hits[:, c * ROWS:(c + 1) * ROWS]
            if c:
                lanes = lanes + e[:, c * ROWS:(c + 1) * ROWS]
        sums.append(jnp.sum(lanes.T, axis=0, keepdims=True))
    first = core == 0
    row = jnp.concatenate([jnp.where(first, sums[0], sums[1]), jnp.where(first, sums[1], sums[0]),
                           jnp.zeros((8 - NC, ROWS), jnp.float32)], axis=0)
    nrow = NCOL // ROWS
    col = jnp.concatenate([colsum[:, c * ROWS:(c + 1) * ROWS] for c in range(nrow)]
                          + [pos, jnp.zeros((7 - nrow, ROWS), jnp.float32)], axis=0)
    row_ref[...] = row
    for k in range(NZ * NYH):
        col_ref[k] = col


def grad_kernel(pos_ref, s_ref, own_ref, oth_ref, cols_ref, ownp_ref, othp_ref, rows_ref, cols_l_ref, mine_ref, theirs_ref, w_hi, w_lo):
    core = pos_ref[1]
    row_l = jnp.sum(rows_ref[...], axis=0)
    col_l = jnp.sum(cols_l_ref[...], axis=0)
    nrow = NCOL // ROWS
    col_inv = jnp.concatenate([1.0 / col_l[c:c + 1, :] for c in range(nrow)], axis=1)
    loss = jnp.sum(jnp.log(col_l[:nrow, :]), axis=0, keepdims=True) - col_l[nrow:nrow + 1, :]
    projs = []
    for j, part in enumerate((ownp_ref, othp_ref)):
        s = s_ref[j * ROWS:(j + 1) * ROWS, :]
        half = core ^ j
        diag, hit = tile_masks(pos_ref, half, part[...])
        inv = column(1.0 / jnp.where(half == 0, row_l[0:1, :], row_l[1:2, :]))
        w = jnp.where(diag, 0.0, jnp.exp(s) * (inv + col_inv)) - jnp.where(hit, 2.0, 0.0)
        projs.append(jnp.sum(w * s, axis=1, keepdims=True))
        w_hi[j], w_lo[j] = split(w)
    weights = (w_hi[...].reshape(NC * ROWS, NCOL), w_lo[...].reshape(NC * ROWS, NCOL))
    step = 2 * FEAT
    tail = jnp.concatenate([loss, jnp.zeros((7, ROWS), jnp.float32)], axis=0)
    for c in range(WIDE // step):
        at = slice(c * step, (c + 1) * step)
        g = INV_TAU * dot3(weights, split(cols_ref[:, at]), ((1,), (0,)))
        for j, (units, out) in enumerate(((own_ref, mine_ref), (oth_ref, theirs_ref))):
            t = (g[j * ROWS:(j + 1) * ROWS, :] - units[:, at] * projs[j]).T
            for p in range(2):
                out[2 * c + p, :FEAT, :] = t[p * FEAT:(p + 1) * FEAT, :]
                out[2 * c + p, FEAT:, :] = tail


def last_kernel(piece_ref, scale_ref, loss_ref, grad_ref):
    total = jnp.sum(piece_ref[...], axis=0)
    loss_ref[...] = jnp.sum(total[FEAT:FEAT + 1, :], axis=1, keepdims=True) / TOTAL
    grad_ref[...] = total[:FEAT, :] * scale_ref[...]


def swap(x, axes, size, k):
    return lax.ppermute(x, axes, [(i, i ^ k) for i in range(size)])


def trade(x, axes):
    return lax.all_to_all(x, axes, 0, 0, tiled=True)


def call(body, name, outs, args, scratch=(), far=(), limit=24):
    return pl.pallas_call(
        body,
        out_shape=outs,
        in_specs=[SMEM if a.shape == (3,) else HBM if i in far else VMEM for i, a in enumerate(args)],
        out_specs=[VMEM] * len(outs),
        scratch_shapes=list(scratch),
        compiler_params=pltpu.CompilerParams(vmem_limit_bytes=limit * MIB),
        name=name,
    )(*args)


def per_device(views, partner):
    zy = lax.axis_index(("z", "yh"))
    core = lax.axis_index("core")
    me = lax.axis_index(("yl", "x"))
    pos = jnp.stack([zy, core, me]).astype(jnp.int32)
    feat = ("yl", "x")

    own_p = partner.reshape(ROWS, 1)
    oth_p = swap(partner, "core", NC, 1).reshape(ROWS, 1)
    packed = CHUNK * FEAT // ROWS
    whole = lax.all_gather(views.T, feat, axis=0, tiled=True)
    chunks, = call(chunk_kernel, "chunks", [f32(NYH * NF, packed, ROWS)], [views.T])
    chunk, = call(column_kernel, "columns", [f32(NYH * CHUNK, WIDE)], [trade(chunks, ("yh", "yl", "x"))])
    cols = lax.all_gather(chunk, "z", axis=0, tiled=True)
    own, scale = call(norm_kernel, "norm", [f32(ROWS, WIDE), f32(1, ROWS)], [whole])
    oth = swap(own, "core", NC, 1)
    s, row, col = call(
        score_kernel, "scores",
        [f32(NC * ROWS, NCOL), f32(8, ROWS), f32(NZ * NYH, 8, ROWS)],
        [pos, own, oth, cols, own_p, oth_p],
        [pltpu.VMEM((NC, ROWS, WIDE), jnp.bfloat16)] * 2
        + [pltpu.VMEM((NCOL, WIDE), jnp.float32), pltpu.SemaphoreType.DMA((NCOL // 256,))],
        far=(3,), limit=48,
    )
    rows_l = lax.all_gather(row, ("core", "yl", "x"), axis=0, tiled=False)
    cols_l = trade(col, ("z", "yh"))
    mine, theirs = call(
        grad_kernel, "gradient",
        [f32(NF, PIECE, ROWS)] * 2,
        [pos, s, own, oth, cols, own_p, oth_p, rows_l, cols_l],
        [pltpu.VMEM((NC, ROWS, NCOL), jnp.bfloat16)] * 2,
    )
    pieces = trade(mine + swap(theirs, "core", NC, 1), feat)
    loss, grad = call(last_kernel, "finish", [f32(1, 1), f32(FEAT, ROWS)], [pieces, scale])
    return loss.reshape(()), grad.T


def solution(mesh):
    fine = Mesh(mesh.devices.reshape(NZ, NYH, NC, NYL, NX), ("z", "yh", "core", "yl", "x"))
    rows = ("z", "yh", "core")
    return jax.shard_map(
        per_device,
        mesh=fine,
        in_specs=(P(rows, ("yl", "x")), P(rows)),
        out_specs=(P(), P(rows, ("yl", "x"))),
        check_vma=False,
    )
```

```python
import jax
import jax.numpy as jnp
from jax import lax
from jax.experimental import pallas as pl
from jax.experimental.pallas import tpu as pltpu
from jax.sharding import Mesh, PartitionSpec as P

NZ, NYH, NC, NYL, NX = 8, 4, 2, 2, 4
NF = NYL * NX
ROWS = 128
FEAT = 192
WIDE = NF * FEAT
CHUNK = ROWS // NF
NCOL = NZ * NYH * CHUNK
PIECE = FEAT + 8
TOTAL = 8192
INV_TAU = 10.0
VMEM = pl.BlockSpec(memory_space=pltpu.VMEM)
SMEM = pl.BlockSpec(memory_space=pltpu.SMEM)
PARAMS = pltpu.CompilerParams(vmem_limit_bytes=32 * 1024 * 1024)


def f32(*shape):
    return jax.ShapeDtypeStruct(shape, jnp.float32)


def split(x):
    hi = x.astype(jnp.bfloat16)
    lo = (x - hi.astype(jnp.float32)).astype(jnp.bfloat16)
    return hi, lo


def dot3(a, b, dims):
    def one(x, y):
        return lax.dot_general(x, y, (dims, ((), ())), preferred_element_type=jnp.float32)
    return one(a[0], b[0]) + (one(a[0], b[1]) + one(a[1], b[0]))


def column(x):
    return jnp.broadcast_to(x, (ROWS, ROWS)).T[:, :1]


def pack(x):
    half = CHUNK // 2
    return jnp.concatenate([x[:, :ROWS], jnp.concatenate([x[:half, ROWS:], x[half:, ROWS:]], axis=1)], axis=0)


def unpack(x):
    tail = x[CHUNK:, :]
    rest = FEAT - ROWS
    return jnp.concatenate([x[:CHUNK, :], jnp.concatenate([tail[:, :rest], tail[:, rest:]], axis=0)], axis=1)


def chunk_kernel(view_ref, out_ref):
    x = view_ref[...].T
    for f in range(NF):
        piece = pack(x[f * CHUNK:(f + 1) * CHUNK, :])
        for y in range(NYH):
            out_ref[y * NF + f] = piece


def column_kernel(piece_ref, view_ref, unit_ref, copies_ref):
    for y in range(NYH):
        x = jnp.concatenate([unpack(piece_ref[y * NF + f]) for f in range(NF)], axis=1)
        scale = lax.rsqrt(jnp.sum(x * x, axis=1, keepdims=True) + 1e-06)
        unit_ref[y * CHUNK:(y + 1) * CHUNK, :] = x * scale
    for f in range(NF):
        copies_ref[f] = view_ref[...]


def norm_kernel(piece_ref, unit_ref, scale_ref):
    x = piece_ref[...].reshape(WIDE, ROWS)
    scale = lax.rsqrt(jnp.sum(x * x, axis=0, keepdims=True) + 1e-06)
    scale_ref[...] = scale
    unit_ref[...] = (x * scale).T


def tile_masks(pos_ref, half, part):
    zy, core, me = pos_ref[0], pos_ref[1], pos_ref[2]
    lane = lax.broadcasted_iota(jnp.int32, (1, NCOL), 1)
    col = ((lane // CHUNK) * NC + core) * ROWS + me * CHUNK + lane % CHUNK
    row = (zy * NC + half) * ROWS + lax.broadcasted_iota(jnp.int32, (ROWS, 1), 0)
    return col == row, col == part


def score_kernel(pos_ref, own_ref, oth_ref, cols_ref, ownp_ref, othp_ref, s_ref, row_ref, col_ref, hi, lo):
    core = pos_ref[1]
    for j, ref in enumerate((own_ref, oth_ref)):
        hi[j], lo[j] = split(ref[...])
    rows = (hi[...].reshape(NC * ROWS, WIDE), lo[...].reshape(NC * ROWS, WIDE))
    step = 256
    for c in range(0, NCOL, step):
        s_ref[:, c:c + step] = INV_TAU * dot3(rows, split(cols_ref[c:c + step, :]), ((1,), (1,)))
    colsum = jnp.zeros((1, NCOL), jnp.float32)
    pos = jnp.zeros((1, ROWS), jnp.float32)
    sums = []
    for j, part in enumerate((ownp_ref, othp_ref)):
        s = s_ref[j * ROWS:(j + 1) * ROWS, :]
        diag, hit = tile_masks(pos_ref, core ^ j, part[...])
        e = jnp.where(diag, 0.0, jnp.exp(s))
        colsum = colsum + jnp.sum(e, axis=0, keepdims=True)
        lanes = e[:, :ROWS]
        hits = jnp.sum(jnp.where(hit, s, 0.0), axis=0, keepdims=True)
        for c in range(NCOL // ROWS):
            pos = pos + hits[:, c * ROWS:(c + 1) * ROWS]
            if c:
                lanes = lanes + e[:, c * ROWS:(c + 1) * ROWS]
        sums.append(jnp.sum(lanes.T, axis=0, keepdims=True))
    first = core == 0
    row = jnp.concatenate([jnp.where(first, sums[0], sums[1]), jnp.where(first, sums[1], sums[0]),
                           jnp.zeros((8 - NC, ROWS), jnp.float32)], axis=0)
    nrow = NCOL // ROWS
    col = jnp.concatenate([colsum[:, c * ROWS:(c + 1) * ROWS] for c in range(nrow)]
                          + [pos, jnp.zeros((7 - nrow, ROWS), jnp.float32)], axis=0)
    row_ref[...] = row
    for k in range(NZ * NYH):
        col_ref[k] = col


def split_kernel(cols_ref, row_ref, hi_ref, lo_ref):
    step = 128
    for c in range(0, NCOL, step):
        h, l = split(cols_ref[c:c + step, :])
        hi_ref[c:c + step, :] = h
        lo_ref[c:c + step, :] = l


def grad_kernel(pos_ref, s_ref, own_ref, oth_ref, chi_ref, clo_ref, ownp_ref, othp_ref, rows_ref, cols_l_ref, mine_ref, theirs_ref, w_hi, w_lo):
    core = pos_ref[1]
    row_l = rows_ref[...]
    col_l = jnp.sum(cols_l_ref[...], axis=0)
    nrow = NCOL // ROWS
    col_inv = jnp.concatenate([1.0 / col_l[c:c + 1, :] for c in range(nrow)], axis=1)
    loss = jnp.sum(jnp.log(col_l[:nrow, :]), axis=0, keepdims=True) - col_l[nrow:nrow + 1, :]
    projs = []
    for j, part in enumerate((ownp_ref, othp_ref)):
        s = s_ref[j * ROWS:(j + 1) * ROWS, :]
        half = core ^ j
        diag, hit = tile_masks(pos_ref, half, part[...])
        inv = column(1.0 / jnp.where(half == 0, row_l[0:1, :], row_l[1:2, :]))
        w = jnp.where(diag, 0.0, jnp.exp(s) * (inv + col_inv)) - jnp.where(hit, 2.0, 0.0)
        projs.append(jnp.sum(w * s, axis=1, keepdims=True))
        w_hi[j], w_lo[j] = split(w)
    weights = (w_hi[...].reshape(NC * ROWS, NCOL), w_lo[...].reshape(NC * ROWS, NCOL))
    step = 2 * FEAT
    tail = jnp.concatenate([loss, jnp.zeros((7, ROWS), jnp.float32)], axis=0)
    for c in range(WIDE // step):
        at = slice(c * step, (c + 1) * step)
        g = INV_TAU * dot3(weights, (chi_ref[:, at], clo_ref[:, at]), ((1,), (0,)))
        for j, (units, out) in enumerate(((own_ref, mine_ref), (oth_ref, theirs_ref))):
            t = (g[j * ROWS:(j + 1) * ROWS, :] - units[:, at] * projs[j]).T
            for p in range(2):
                out[2 * c + p, :FEAT, :] = t[p * FEAT:(p + 1) * FEAT, :]
                out[2 * c + p, FEAT:, :] = tail


def last_kernel(piece_ref, scale_ref, loss_ref, grad_ref):
    total = jnp.sum(piece_ref[...], axis=0)
    loss_ref[...] = jnp.sum(total[FEAT:FEAT + 1, :], axis=1, keepdims=True) / TOTAL
    grad_ref[...] = total[:FEAT, :] * scale_ref[...]


def swap(x, axes, size, k):
    return lax.ppermute(x, axes, [(i, i ^ k) for i in range(size)])


def trade(x, axes):
    return lax.all_to_all(x, axes, 0, 0, tiled=True)


def call(body, name, outs, args, scratch=()):
    return pl.pallas_call(
        body,
        out_shape=outs,
        in_specs=[SMEM if a.shape == (3,) else VMEM for a in args],
        out_specs=[VMEM] * len(outs),
        scratch_shapes=list(scratch),
        compiler_params=PARAMS,
        name=name,
    )(*args)


def per_device(views, partner):
    zy = lax.axis_index(("z", "yh"))
    core = lax.axis_index("core")
    me = lax.axis_index(("yl", "x"))
    pos = jnp.stack([zy, core, me]).astype(jnp.int32)
    feat = ("yl", "x")

    own_p = partner.reshape(ROWS, 1)
    oth_p = swap(partner, "core", NC, 1).reshape(ROWS, 1)
    packed = CHUNK * FEAT // ROWS
    chunks, = call(chunk_kernel, "chunks", [f32(NYH * NF, packed, ROWS)], [views.T])
    chunks = trade(chunks, ("yh", "yl", "x"))
    chunk, copies = call(column_kernel, "columns", [f32(NYH * CHUNK, WIDE), f32(NF, FEAT, ROWS)], [chunks, views.T])
    cols = lax.all_gather(chunk, "z", axis=0, tiled=True)
    own, scale = call(norm_kernel, "norm", [f32(ROWS, WIDE), f32(1, ROWS)], [trade(copies, feat)])
    oth = swap(own, "core", NC, 1)
    s, row, col = call(
        score_kernel, "scores",
        [f32(NC * ROWS, NCOL), f32(8, ROWS), f32(NZ * NYH, 8, ROWS)],
        [pos, own, oth, cols, own_p, oth_p],
        [pltpu.VMEM((NC, ROWS, WIDE), jnp.bfloat16)] * 2,
    )
    cols_l = trade(col, ("z", "yh"))
    bf16 = jax.ShapeDtypeStruct((NCOL, WIDE), jnp.bfloat16)
    chi, clo = call(split_kernel, "split", [bf16] * 2, [cols, row])
    rows_l = row
    for axis, size, k in (("core", NC, 1), ("x", NX, 1), ("x", NX, 2), ("yl", NYL, 1)):
        rows_l = rows_l + swap(rows_l, axis, size, k)
    mine, theirs = call(
        grad_kernel, "gradient",
        [f32(NF, PIECE, ROWS)] * 2,
        [pos, s, own, oth, chi, clo, own_p, oth_p, rows_l, cols_l],
        [pltpu.VMEM((NC, ROWS, NCOL), jnp.bfloat16)] * 2,
    )
    pieces = trade(mine + swap(theirs, "core", NC, 1), feat)
    loss, grad = call(last_kernel, "finish", [f32(1, 1), f32(FEAT, ROWS)], [pieces, scale])
    return loss.reshape(()), grad.T


def solution(mesh):
    fine = Mesh(mesh.devices.reshape(NZ, NYH, NC, NYL, NX), ("z", "yh", "core", "yl", "x"))
    rows = ("z", "yh", "core")
    return jax.shard_map(
        per_device,
        mesh=fine,
        in_specs=(P(rows, ("yl", "x")), P(rows)),
        out_specs=(P(), P(rows, ("yl", "x"))),
        check_vma=False,
    )
```

```python
import jax
import jax.numpy as jnp
from jax import lax
from jax.experimental import pallas as pl
from jax.experimental.pallas import tpu as pltpu
from jax.sharding import Mesh, PartitionSpec as P

NZ, NYH, NC, NYL, NX = 8, 4, 2, 2, 4
NF = NYL * NX
ROWS = 128
FEAT = 192
WIDE = NF * FEAT
CHUNK = ROWS // NF
NCOL = NZ * NYH * CHUNK
PIECE = FEAT
NDP = NZ * NYH * NC
TOTAL = 8192
INV_TAU = 10.0
VMEM = pl.BlockSpec(memory_space=pltpu.VMEM)
SMEM = pl.BlockSpec(memory_space=pltpu.SMEM)
PARAMS = pltpu.CompilerParams(vmem_limit_bytes=48 * 1024 * 1024)


def f32(*shape):
    return jax.ShapeDtypeStruct(shape, jnp.float32)


def split(x):
    hi = x.astype(jnp.bfloat16)
    lo = (x - hi.astype(jnp.float32)).astype(jnp.bfloat16)
    return hi, lo


def dot3(a, b, dims):
    def one(x, y):
        return lax.dot_general(x, y, (dims, ((), ())), preferred_element_type=jnp.float32)
    return one(a[0], b[0]) + (one(a[0], b[1]) + one(a[1], b[0]))


def column(x):
    return jnp.broadcast_to(x, (ROWS, ROWS)).T[:, :1]


def pack(x):
    half = CHUNK // 2
    return jnp.concatenate([x[:, :ROWS], jnp.concatenate([x[:half, ROWS:], x[half:, ROWS:]], axis=1)], axis=0)


def unpack(x):
    tail = x[CHUNK:, :]
    rest = FEAT - ROWS
    return jnp.concatenate([x[:CHUNK, :], jnp.concatenate([tail[:, :rest], tail[:, rest:]], axis=0)], axis=1)


def chunk_kernel(view_ref, out_ref):
    x = view_ref[...].T
    for f in range(NF):
        piece = pack(x[f * CHUNK:(f + 1) * CHUNK, :])
        for y in range(NYH):
            out_ref[y * NF + f] = piece


def column_kernel(piece_ref, view_ref, unit_ref, copies_ref):
    for y in range(NYH):
        x = jnp.concatenate([unpack(piece_ref[y * NF + f]) for f in range(NF)], axis=1)
        scale = lax.rsqrt(jnp.sum(x * x, axis=1, keepdims=True) + 1e-06)
        unit_ref[y * CHUNK:(y + 1) * CHUNK, :] = x * scale
    for f in range(NF):
        copies_ref[f] = view_ref[...]


def norm_kernel(piece_ref, unit_ref, scale_ref):
    x = piece_ref[...].reshape(WIDE, ROWS)
    scale = lax.rsqrt(jnp.sum(x * x, axis=0, keepdims=True) + 1e-06)
    scale_ref[...] = scale
    unit_ref[...] = (x * scale).T


def tile_masks(pos_ref, half, part):
    zy, core, me = pos_ref[0], pos_ref[1], pos_ref[2]
    lane = lax.broadcasted_iota(jnp.int32, (1, NCOL), 1)
    col = ((lane // CHUNK) * NC + core) * ROWS + me * CHUNK + lane % CHUNK
    row = (zy * NC + half) * ROWS + lax.broadcasted_iota(jnp.int32, (ROWS, 1), 0)
    return col == row, col == part


def score_kernel(pos_ref, own_ref, oth_ref, cols_ref, ownp_ref, othp_ref, s_ref, sum_ref, hi, lo):
    core = pos_ref[1]
    for j, ref in enumerate((own_ref, oth_ref)):
        hi[j], lo[j] = split(ref[...])
    rows = (hi[...].reshape(NC * ROWS, WIDE), lo[...].reshape(NC * ROWS, WIDE))
    step = 256
    for c in range(0, NCOL, step):
        s_ref[:, c:c + step] = INV_TAU * dot3(rows, split(cols_ref[c:c + step, :]), ((1,), (1,)))
    pos = jnp.zeros((1, ROWS), jnp.float32)
    sum_ref[...] = jnp.zeros((NDP + 8, ROWS), jnp.float32)
    for j, part in enumerate((ownp_ref, othp_ref)):
        s = s_ref[j * ROWS:(j + 1) * ROWS, :]
        diag, hit = tile_masks(pos_ref, core ^ j, part[...])
        e = jnp.where(diag, 0.0, jnp.exp(s))
        hits = jnp.sum(jnp.where(hit, s, 0.0), axis=0, keepdims=True)
        lanes = e[:, :ROWS]
        for c in range(NCOL // ROWS):
            pos = pos + hits[:, c * ROWS:(c + 1) * ROWS]
            if c:
                lanes = lanes + e[:, c * ROWS:(c + 1) * ROWS]
        sum_ref[pl.ds(pos_ref[0] * NC + (core ^ j), 1), :] = jnp.sum(lanes.T, axis=0, keepdims=True)
    sum_ref[NDP:NDP + 1, :] = pos


def grad_kernel(pos_ref, s_ref, own_ref, oth_ref, cols_ref, ownp_ref, othp_ref, sum_ref, mine_ref, theirs_ref, loss_ref, w_hi, w_lo):
    core = pos_ref[1]
    zy, me = pos_ref[0], pos_ref[2]
    every = sum_ref[:NDP, :]
    logs = jnp.sum(jnp.log(every), axis=0, keepdims=True) - sum_ref[NDP:NDP + 1, :]
    loss_ref[...] = jnp.sum(logs, axis=1, keepdims=True) / TOTAL
    dp = lax.broadcasted_iota(jnp.int32, (NDP, NCOL), 0)
    lane = lax.broadcasted_iota(jnp.int32, (NDP, NCOL), 1)
    source = lax.broadcasted_iota(jnp.int32, (ROWS, NCOL), 0)
    target = lax.broadcasted_iota(jnp.int32, (ROWS, NCOL), 1)
    pick = jnp.where(source == me * CHUNK + target % CHUNK, 1.0, 0.0)
    spread = lax.dot_general(1.0 / every, pick, (((1,), (0,)), ((), ())), precision=lax.Precision.HIGHEST,
                             preferred_element_type=jnp.float32)
    col_inv = jnp.sum(jnp.where(dp == (lane // CHUNK) * NC + core, spread, 0.0), axis=0, keepdims=True)
    projs = []
    for j, part in enumerate((ownp_ref, othp_ref)):
        s = s_ref[j * ROWS:(j + 1) * ROWS, :]
        half = core ^ j
        diag, hit = tile_masks(pos_ref, half, part[...])
        inv = column(1.0 / sum_ref[pl.ds(zy * NC + half, 1), :])
        w = jnp.where(diag, 0.0, jnp.exp(s) * (inv + col_inv)) - jnp.where(hit, 2.0, 0.0)
        projs.append(jnp.sum(w * s, axis=1, keepdims=True))
        w_hi[j], w_lo[j] = split(w)
    weights = (w_hi[...].reshape(NC * ROWS, NCOL), w_lo[...].reshape(NC * ROWS, NCOL))
    step = 2 * FEAT
    for c in range(WIDE // step):
        at = slice(c * step, (c + 1) * step)
        g = INV_TAU * dot3(weights, split(cols_ref[:, at]), ((1,), (0,)))
        for j, (units, out) in enumerate(((own_ref, mine_ref), (oth_ref, theirs_ref))):
            t = (g[j * ROWS:(j + 1) * ROWS, :] - units[:, at] * projs[j]).T
            for p in range(2):
                out[2 * c + p] = t[p * FEAT:(p + 1) * FEAT, :]


def last_kernel(piece_ref, scale_ref, grad_ref):
    grad_ref[...] = jnp.sum(piece_ref[...], axis=0) * scale_ref[...]


def swap(x, axes, size, k):
    return lax.ppermute(x, axes, [(i, i ^ k) for i in range(size)])


def trade(x, axes):
    return lax.all_to_all(x, axes, 0, 0, tiled=True)


def call(body, name, outs, args, scratch=()):
    return pl.pallas_call(
        body,
        out_shape=outs,
        in_specs=[SMEM if a.shape == (3,) else VMEM for a in args],
        out_specs=[VMEM] * len(outs),
        scratch_shapes=list(scratch),
        compiler_params=PARAMS,
        name=name,
    )(*args)


def per_device(views, partner):
    zy = lax.axis_index(("z", "yh"))
    core = lax.axis_index("core")
    me = lax.axis_index(("yl", "x"))
    pos = jnp.stack([zy, core, me]).astype(jnp.int32)
    feat = ("yl", "x")

    own_p = partner.reshape(ROWS, 1)
    oth_p = swap(partner, "core", NC, 1).reshape(ROWS, 1)
    packed = CHUNK * FEAT // ROWS
    chunks, = call(chunk_kernel, "chunks", [f32(NYH * NF, packed, ROWS)], [views.T])
    chunks = trade(chunks, ("yh", "yl", "x"))
    chunk, copies = call(column_kernel, "columns", [f32(NYH * CHUNK, WIDE), f32(NF, FEAT, ROWS)], [chunks, views.T])
    cols = lax.all_gather(chunk, "z", axis=0, tiled=True)
    own, scale = call(norm_kernel, "norm", [f32(ROWS, WIDE), f32(1, ROWS)], [trade(copies, feat)])
    oth = swap(own, "core", NC, 1)
    s, sums = call(
        score_kernel, "scores",
        [f32(NC * ROWS, NCOL), f32(NDP + 8, ROWS)],
        [pos, own, oth, cols, own_p, oth_p],
        [pltpu.VMEM((NC, ROWS, WIDE), jnp.bfloat16)] * 2,
    )
    sums = lax.psum(sums, ("z", "yh", "core", "yl", "x"))
    mine, theirs, loss = call(
        grad_kernel, "gradient",
        [f32(NF, PIECE, ROWS)] * 2 + [f32(1, 1)],
        [pos, s, own, oth, cols, own_p, oth_p, sums],
        [pltpu.VMEM((NC, ROWS, NCOL), jnp.bfloat16)] * 2,
    )
    pieces = trade(mine + swap(theirs, "core", NC, 1), feat)
    grad, = call(last_kernel, "finish", [f32(FEAT, ROWS)], [pieces, scale])
    return loss.reshape(()), grad.T


def solution(mesh):
    fine = Mesh(mesh.devices.reshape(NZ, NYH, NC, NYL, NX), ("z", "yh", "core", "yl", "x"))
    rows = ("z", "yh", "core")
    return jax.shard_map(
        per_device,
        mesh=fine,
        in_specs=(P(rows, ("yl", "x")), P(rows)),
        out_specs=(P(), P(rows, ("yl", "x"))),
        check_vma=False,
    )
```

```python
import jax
import jax.numpy as jnp
from jax import lax
from jax.experimental import pallas as pl
from jax.experimental.pallas import tpu as pltpu
from jax.sharding import Mesh, PartitionSpec as P

NZ, NYH, NC, NYL, NX = 8, 4, 2, 2, 4
NF = NYL * NX
ROWS = 128
FEAT = 192
WIDE = NF * FEAT
CHUNK = ROWS // NF
NCOL = NZ * NYH * CHUNK
PIECE = FEAT + 8
SHARE = NYH * CHUNK // 2
PART = NZ * SHARE
TOTAL = 8192
INV_TAU = 10.0
VMEM = pl.BlockSpec(memory_space=pltpu.VMEM)
SMEM = pl.BlockSpec(memory_space=pltpu.SMEM)
PARAMS = pltpu.CompilerParams(vmem_limit_bytes=32 * 1024 * 1024)


def f32(*shape):
    return jax.ShapeDtypeStruct(shape, jnp.float32)


def split(x):
    hi = x.astype(jnp.bfloat16)
    lo = (x - hi.astype(jnp.float32)).astype(jnp.bfloat16)
    return hi, lo


def dot3(a, b, dims):
    def one(x, y):
        return lax.dot_general(x, y, (dims, ((), ())), preferred_element_type=jnp.float32)
    return one(a[0], b[0]) + (one(a[0], b[1]) + one(a[1], b[0]))


def column(x):
    return jnp.broadcast_to(x, (ROWS, ROWS)).T[:, :1]


def pack(x):
    half = CHUNK // 2
    return jnp.concatenate([x[:, :ROWS], jnp.concatenate([x[:half, ROWS:], x[half:, ROWS:]], axis=1)], axis=0)


def unpack(x):
    tail = x[CHUNK:, :]
    rest = FEAT - ROWS
    return jnp.concatenate([x[:CHUNK, :], jnp.concatenate([tail[:, :rest], tail[:, rest:]], axis=0)], axis=1)


def chunk_kernel(view_ref, out_ref):
    x = view_ref[...].T
    for f in range(NF):
        piece = pack(x[f * CHUNK:(f + 1) * CHUNK, :])
        for y in range(NYH):
            out_ref[y * NF + f] = piece


def column_kernel(piece_ref, first_ref, second_ref):
    for y in range(NYH):
        x = jnp.concatenate([unpack(piece_ref[y * NF + f]) for f in range(NF)], axis=1)
        scale = lax.rsqrt(jnp.sum(x * x, axis=1, keepdims=True) + 1e-06)
        out, at = (first_ref, y) if y < NYH // 2 else (second_ref, y - NYH // 2)
        out[at * CHUNK:(at + 1) * CHUNK, :] = x * scale


def norm_kernel(pos_ref, piece_ref, own_ref, oth_ref, scale_ref):
    core = pos_ref[1]
    for j, out in enumerate((own_ref, oth_ref)):
        x = piece_ref[core ^ j]
        scale = lax.rsqrt(jnp.sum(x * x, axis=0, keepdims=True) + 1e-06)
        if j == 0:
            scale_ref[...] = scale
        out[...] = (x * scale).T


def tile_masks(pos_ref, half, part):
    zy, core, me = pos_ref[0], pos_ref[1], pos_ref[2]
    lane = lax.broadcasted_iota(jnp.int32, (1, NCOL), 1)
    y = (lane // PART) * (NYH // 2) + (lane % SHARE) // CHUNK
    z = (lane % PART) // SHARE
    col = ((z * NYH + y) * NC + core) * ROWS + me * CHUNK + lane % CHUNK
    row = (zy * NC + half) * ROWS + lax.broadcasted_iota(jnp.int32, (ROWS, 1), 0)
    return col == row, col == part


def score_kernel(pos_ref, own_ref, oth_ref, first_ref, ownp_ref, othp_ref, *refs):
    blocks, (s_ref, row_ref, col_ref, second_ref, hi, lo) = refs[:NZ], refs[NZ:]
    core = pos_ref[1]
    z = pos_ref[0] // NYH
    for k, block in enumerate(blocks):
        at = pl.multiple_of(((z + NZ - k) % NZ) * SHARE, SHARE)
        second_ref[pl.ds(at, SHARE), :] = block[...]
    for j, ref in enumerate((own_ref, oth_ref)):
        hi[j], lo[j] = split(ref[...])
    rows = (hi[...].reshape(NC * ROWS, WIDE), lo[...].reshape(NC * ROWS, WIDE))
    for i, ref in enumerate((first_ref, second_ref)):
        s_ref[:, i * PART:(i + 1) * PART] = INV_TAU * dot3(rows, split(ref[...]), ((1,), (1,)))
    colsum = jnp.zeros((1, NCOL), jnp.float32)
    pos = jnp.zeros((1, ROWS), jnp.float32)
    sums = []
    for j, part in enumerate((ownp_ref, othp_ref)):
        s = s_ref[j * ROWS:(j + 1) * ROWS, :]
        diag, hit = tile_masks(pos_ref, core ^ j, part[...])
        e = jnp.where(diag, 0.0, jnp.exp(s))
        colsum = colsum + jnp.sum(e, axis=0, keepdims=True)
        lanes = e[:, :ROWS]
        hits = jnp.sum(jnp.where(hit, s, 0.0), axis=0, keepdims=True)
        for c in range(NCOL // ROWS):
            pos = pos + hits[:, c * ROWS:(c + 1) * ROWS]
            if c:
                lanes = lanes + e[:, c * ROWS:(c + 1) * ROWS]
        sums.append(jnp.sum(lanes.T, axis=0, keepdims=True))
    first = core == 0
    row = jnp.concatenate([jnp.where(first, sums[0], sums[1]), jnp.where(first, sums[1], sums[0]),
                           jnp.zeros((8 - NC, ROWS), jnp.float32)], axis=0)
    nrow = NCOL // ROWS
    col = jnp.concatenate([colsum[:, c * ROWS:(c + 1) * ROWS] for c in range(nrow)]
                          + [pos, jnp.zeros((7 - nrow, ROWS), jnp.float32)], axis=0)
    for k in range(NC * NF):
        row_ref[k] = row
    for k in range(NZ * NYH):
        col_ref[k] = col


def grad_kernel(pos_ref, s_ref, own_ref, oth_ref, first_ref, second_ref, ownp_ref, othp_ref, rows_ref, cols_l_ref, mine_ref, theirs_ref, w_hi, w_lo):
    core = pos_ref[1]
    row_l = jnp.sum(rows_ref[...], axis=0)
    col_l = jnp.sum(cols_l_ref[...], axis=0)
    nrow = NCOL // ROWS
    col_inv = jnp.concatenate([1.0 / col_l[c:c + 1, :] for c in range(nrow)], axis=1)
    loss = jnp.sum(jnp.log(col_l[:nrow, :]), axis=0, keepdims=True) - col_l[nrow:nrow + 1, :]
    projs = []
    for j, part in enumerate((ownp_ref, othp_ref)):
        s = s_ref[j * ROWS:(j + 1) * ROWS, :]
        half = core ^ j
        diag, hit = tile_masks(pos_ref, half, part[...])
        inv = column(1.0 / jnp.where(half == 0, row_l[0:1, :], row_l[1:2, :]))
        w = jnp.where(diag, 0.0, jnp.exp(s) * (inv + col_inv)) - jnp.where(hit, 2.0, 0.0)
        projs.append(jnp.sum(w * s, axis=1, keepdims=True))
        w_hi[j], w_lo[j] = split(w)
    weights = (w_hi[...].reshape(NC * ROWS, NCOL), w_lo[...].reshape(NC * ROWS, NCOL))
    step = 2 * FEAT
    cols = (first_ref, second_ref)
    tail = jnp.concatenate([loss, jnp.zeros((7, ROWS), jnp.float32)], axis=0)
    for c in range(WIDE // step):
        at = slice(c * step, (c + 1) * step)
        g = INV_TAU * sum(
            dot3([w[:, i * PART:(i + 1) * PART] for w in weights], split(ref[:, at]), ((1,), (0,)))
            for i, ref in enumerate(cols)
        )
        for j, (units, out) in enumerate(((own_ref, mine_ref), (oth_ref, theirs_ref))):
            t = (g[j * ROWS:(j + 1) * ROWS, :] - units[:, at] * projs[j]).T
            for p in range(2):
                out[2 * c + p, :FEAT, :] = t[p * FEAT:(p + 1) * FEAT, :]
                out[2 * c + p, FEAT:, :] = tail


def last_kernel(piece_ref, scale_ref, loss_ref, grad_ref):
    total = jnp.sum(piece_ref[...], axis=0)
    loss_ref[...] = jnp.sum(total[FEAT:FEAT + 1, :], axis=1, keepdims=True) / TOTAL
    grad_ref[...] = total[:FEAT, :] * scale_ref[...]


def swap(x, axes, size, k):
    return lax.ppermute(x, axes, [(i, i ^ k) for i in range(size)])


def around(x):
    blocks = {0: x}
    up = down = x
    for k in range(1, NZ // 2 + 1):
        up = lax.ppermute(up, "z", [(i, (i + 1) % NZ) for i in range(NZ)])
        blocks[k] = up
        if k < NZ // 2:
            down = lax.ppermute(down, "z", [(i, (i - 1) % NZ) for i in range(NZ)])
            blocks[NZ - k] = down
    return [blocks[k] for k in range(NZ)]


def trade(x, axes):
    return lax.all_to_all(x, axes, 0, 0, tiled=True)


def call(body, name, outs, args, scratch=()):
    return pl.pallas_call(
        body,
        out_shape=outs,
        in_specs=[SMEM if a.shape == (3,) else VMEM for a in args],
        out_specs=[VMEM] * len(outs),
        scratch_shapes=list(scratch),
        compiler_params=PARAMS,
        name=name,
    )(*args)


def per_device(views, partner):
    zy = lax.axis_index(("z", "yh"))
    core = lax.axis_index("core")
    me = lax.axis_index(("yl", "x"))
    pos = jnp.stack([zy, core, me]).astype(jnp.int32)
    feat = ("yl", "x")

    own_p = partner.reshape(ROWS, 1)
    oth_p = swap(partner, "core", NC, 1).reshape(ROWS, 1)
    whole = lax.all_gather(views.T, ("core", "yl", "x"), axis=0, tiled=True)
    packed = CHUNK * FEAT // ROWS
    chunks, = call(chunk_kernel, "chunks", [f32(NYH * NF, packed, ROWS)], [views.T])
    chunks = trade(chunks, ("yh", "yl", "x"))
    first, second = call(column_kernel, "columns", [f32(SHARE, WIDE)] * 2, [chunks])
    cols = lax.all_gather(first, "z", axis=0, tiled=True)
    ring = around(second)
    own, oth, scale = call(norm_kernel, "norm", [f32(ROWS, WIDE)] * 2 + [f32(1, ROWS)],
                           [pos, whole.reshape(NC, WIDE, ROWS)])
    s, row, col, rest = call(
        score_kernel, "scores",
        [f32(NC * ROWS, NCOL), f32(NC * NF, 8, ROWS), f32(NZ * NYH, 8, ROWS), f32(PART, WIDE)],
        [pos, own, oth, cols, own_p, oth_p, *ring],
        [pltpu.VMEM((NC, ROWS, WIDE), jnp.bfloat16)] * 2,
    )
    rows_l = trade(row, ("core", "yl", "x"))
    cols_l = trade(col, ("z", "yh"))
    mine, theirs = call(
        grad_kernel, "gradient",
        [f32(NF, PIECE, ROWS)] * 2,
        [pos, s, own, oth, cols, rest, own_p, oth_p, rows_l, cols_l],
        [pltpu.VMEM((NC, ROWS, NCOL), jnp.bfloat16)] * 2,
    )
    pieces = trade(mine + swap(theirs, "core", NC, 1), feat)
    loss, grad = call(last_kernel, "finish", [f32(1, 1), f32(FEAT, ROWS)], [pieces, scale])
    return loss.reshape(()), grad.T


def solution(mesh):
    fine = Mesh(mesh.devices.reshape(NZ, NYH, NC, NYL, NX), ("z", "yh", "core", "yl", "x"))
    rows = ("z", "yh", "core")
    return jax.shard_map(
        per_device,
        mesh=fine,
        in_specs=(P(rows, ("yl", "x")), P(rows)),
        out_specs=(P(), P(rows, ("yl", "x"))),
        check_vma=False,
    )
```

```python
import jax
import jax.numpy as jnp
from jax import lax
from jax.experimental import pallas as pl
from jax.experimental.pallas import tpu as pltpu
from jax.sharding import Mesh, PartitionSpec as P

NZ, NYH, NC, NYL, NX = 8, 4, 2, 2, 4
NF = NYL * NX
ROWS = 128
FEAT = 192
WIDE = NF * FEAT
CHUNK = ROWS // NF
NCOL = NZ * NYH * CHUNK
PIECE = FEAT + 8
PACKED = CHUNK * FEAT // ROWS
ORDER = [low * NX + x for x in range(NX) for low in range(NYL)]
Z = ("zh", "zl")
TOTAL = 8192
INV_TAU = 10.0
VMEM = pl.BlockSpec(memory_space=pltpu.VMEM)
SMEM = pl.BlockSpec(memory_space=pltpu.SMEM)
PARAMS = pltpu.CompilerParams(vmem_limit_bytes=48 * 1024 * 1024)


def f32(*shape):
    return jax.ShapeDtypeStruct(shape, jnp.float32)


def split(x):
    hi = x.astype(jnp.bfloat16)
    lo = (x - hi.astype(jnp.float32)).astype(jnp.bfloat16)
    return hi, lo


def dot3(a, b, dims):
    def one(x, y):
        return lax.dot_general(x, y, (dims, ((), ())), preferred_element_type=jnp.float32)
    return one(a[0], b[0]) + (one(a[0], b[1]) + one(a[1], b[0]))


def column(x):
    return jnp.broadcast_to(x, (ROWS, ROWS)).T[:, :1]


def pack(x):
    half = CHUNK // 2
    return jnp.concatenate([x[:, :ROWS], jnp.concatenate([x[:half, ROWS:], x[half:, ROWS:]], axis=1)], axis=0)


def unpack(x):
    tail = x[CHUNK:, :]
    rest = FEAT - ROWS
    return jnp.concatenate([x[:CHUNK, :], jnp.concatenate([tail[:, :rest], tail[:, rest:]], axis=0)], axis=1)


def chunk_kernel(pos_ref, view_ref, keep_ref, send_ref, copy_ref, held):
    copy_ref[...] = view_ref[...]
    held[...] = view_ref[...].T
    low = pos_ref[2] // NX
    for ref, half in ((keep_ref, low), (send_ref, 1 - low)):
        for x in range(NX):
            at = pl.multiple_of((half * NX + x) * CHUNK, CHUNK)
            ref[x] = pack(held[pl.ds(at, CHUNK), :])


def pair_kernel(pos_ref, kept_ref, got_ref, out_ref):
    first = pos_ref[2] // NX == 0
    for x in range(NX):
        kept, got = kept_ref[x], got_ref[x]
        pair = [unpack(jnp.where(first, kept, got)), unpack(jnp.where(first, got, kept))]
        both = jnp.concatenate(pair, axis=1)
        for y in range(NYH):
            out_ref[y * NX + x] = both


def column_kernel(piece_ref, view_ref, unit_ref, copies_ref):
    for y in range(NYH):
        x = jnp.concatenate([piece_ref[y * NX + k] for k in range(NX)], axis=1)
        scale = lax.rsqrt(jnp.sum(x * x, axis=1, keepdims=True) + 1e-06)
        unit_ref[y * CHUNK:(y + 1) * CHUNK, :] = x * scale
    for f in range(NF):
        copies_ref[f] = view_ref[...]


def norm_kernel(piece_ref, unit_ref, scale_ref):
    x = jnp.concatenate([piece_ref[f] for f in ORDER], axis=0)
    scale = lax.rsqrt(jnp.sum(x * x, axis=0, keepdims=True) + 1e-06)
    scale_ref[...] = scale
    unit_ref[...] = (x * scale).T


def tile_masks(pos_ref, half, part):
    zy, core, me = pos_ref[0], pos_ref[1], pos_ref[2]
    lane = lax.broadcasted_iota(jnp.int32, (1, NCOL), 1)
    col = ((lane // CHUNK) * NC + core) * ROWS + me * CHUNK + lane % CHUNK
    row = (zy * NC + half) * ROWS + lax.broadcasted_iota(jnp.int32, (ROWS, 1), 0)
    return col == row, col == part


def score_kernel(pos_ref, own_ref, oth_ref, cols_ref, ownp_ref, othp_ref, s_ref, row_ref, col_ref, hi, lo):
    core = pos_ref[1]
    for j, ref in enumerate((own_ref, oth_ref)):
        hi[j], lo[j] = split(ref[...])
    rows = (hi[...].reshape(NC * ROWS, WIDE), lo[...].reshape(NC * ROWS, WIDE))
    step = 256
    for c in range(0, NCOL, step):
        s_ref[:, c:c + step] = INV_TAU * dot3(rows, split(cols_ref[c:c + step, :]), ((1,), (1,)))
    colsum = jnp.zeros((1, NCOL), jnp.float32)
    pos = jnp.zeros((1, ROWS), jnp.float32)
    sums = []
    for j, part in enumerate((ownp_ref, othp_ref)):
        s = s_ref[j * ROWS:(j + 1) * ROWS, :]
        diag, hit = tile_masks(pos_ref, core ^ j, part[...])
        e = jnp.where(diag, 0.0, jnp.exp(s))
        colsum = colsum + jnp.sum(e, axis=0, keepdims=True)
        lanes = e[:, :ROWS]
        hits = jnp.sum(jnp.where(hit, s, 0.0), axis=0, keepdims=True)
        for c in range(NCOL // ROWS):
            pos = pos + hits[:, c * ROWS:(c + 1) * ROWS]
            if c:
                lanes = lanes + e[:, c * ROWS:(c + 1) * ROWS]
        sums.append(jnp.sum(lanes.T, axis=0, keepdims=True))
    first = core == 0
    row = jnp.concatenate([jnp.where(first, sums[0], sums[1]), jnp.where(first, sums[1], sums[0]),
                           jnp.zeros((8 - NC, ROWS), jnp.float32)], axis=0)
    nrow = NCOL // ROWS
    col = jnp.concatenate([colsum[:, c * ROWS:(c + 1) * ROWS] for c in range(nrow)]
                          + [pos, jnp.zeros((7 - nrow, ROWS), jnp.float32)], axis=0)
    row_ref[...] = row
    col_ref[...] = col


def relay_kernel(row_a, row_b, col_a, col_b, row_ref, col_ref):
    row = row_a[...] + row_b[...]
    col = col_a[...] + col_b[...]
    for k in range(NF):
        row_ref[k] = row
    for k in range(NZ // 2 * NYH):
        col_ref[k] = col


def grad_kernel(pos_ref, s_ref, own_ref, oth_ref, cols_ref, ownp_ref, othp_ref, rows_ref, cols_l_ref, mine_ref, theirs_ref, w_hi, w_lo):
    core = pos_ref[1]
    row_l = jnp.sum(rows_ref[...], axis=0)
    col_l = jnp.sum(cols_l_ref[...], axis=0)
    nrow = NCOL // ROWS
    col_inv = jnp.concatenate([1.0 / col_l[c:c + 1, :] for c in range(nrow)], axis=1)
    loss = jnp.sum(jnp.log(col_l[:nrow, :]), axis=0, keepdims=True) - col_l[nrow:nrow + 1, :]
    projs = []
    for j, part in enumerate((ownp_ref, othp_ref)):
        s = s_ref[j * ROWS:(j + 1) * ROWS, :]
        half = core ^ j
        diag, hit = tile_masks(pos_ref, half, part[...])
        inv = column(1.0 / jnp.where(half == 0, row_l[0:1, :], row_l[1:2, :]))
        w = jnp.where(diag, 0.0, jnp.exp(s) * (inv + col_inv)) - jnp.where(hit, 2.0, 0.0)
        projs.append(jnp.sum(w * s, axis=1, keepdims=True))
        w_hi[j], w_lo[j] = split(w)
    weights = (w_hi[...].reshape(NC * ROWS, NCOL), w_lo[...].reshape(NC * ROWS, NCOL))
    step = 4 * FEAT
    tail = jnp.concatenate([loss, jnp.zeros((7, ROWS), jnp.float32)], axis=0)
    for c in range(WIDE // step):
        at = slice(c * step, (c + 1) * step)
        g = INV_TAU * dot3(weights, split(cols_ref[:, at]), ((1,), (0,)))
        for j, (units, out) in enumerate(((own_ref, mine_ref), (oth_ref, theirs_ref))):
            t = (g[j * ROWS:(j + 1) * ROWS, :] - units[:, at] * projs[j]).T
            for p in range(4):
                out[ORDER[4 * c + p], :FEAT, :] = t[p * FEAT:(p + 1) * FEAT, :]
                out[ORDER[4 * c + p], FEAT:, :] = tail


def last_kernel(piece_ref, scale_ref, loss_ref, grad_ref):
    total = jnp.sum(piece_ref[...], axis=0)
    loss_ref[...] = jnp.sum(total[FEAT:FEAT + 1, :], axis=1, keepdims=True) / TOTAL
    grad_ref[...] = total[:FEAT, :] * scale_ref[...]


def swap(x, axes, size, k):
    return lax.ppermute(x, axes, [(i, i ^ k) for i in range(size)])


def trade(x, axes):
    return lax.all_to_all(x, axes, 0, 0, tiled=True)


def call(body, name, outs, args, scratch=()):
    return pl.pallas_call(
        body,
        out_shape=outs,
        in_specs=[SMEM if a.shape == (3,) else VMEM for a in args],
        out_specs=[VMEM] * len(outs),
        scratch_shapes=list(scratch),
        compiler_params=PARAMS,
        name=name,
    )(*args)


def per_device(views, partner):
    zy = lax.axis_index(Z + ("yh",))
    core = lax.axis_index("core")
    me = lax.axis_index(("yl", "x"))
    pos = jnp.stack([zy, core, me]).astype(jnp.int32)
    feat = ("yl", "x")

    own_p = partner.reshape(ROWS, 1)
    oth_p = swap(partner, "core", NC, 1).reshape(ROWS, 1)
    keep, send, copy = call(chunk_kernel, "chunks", [f32(NX, PACKED, ROWS)] * 2 + [f32(FEAT, ROWS)], [pos, views.T],
                      [pltpu.VMEM((ROWS, FEAT), jnp.float32)])
    pairs, = call(pair_kernel, "pairs", [f32(NYH * NX, CHUNK, 2 * FEAT)], [pos, keep, swap(send, "yl", NYL, 1)])
    chunk, copies = call(column_kernel, "columns", [f32(NYH * CHUNK, WIDE), f32(NF, FEAT, ROWS)],
                         [trade(pairs, ("yh", "x")), copy])
    cols = lax.all_gather(chunk, Z, axis=0, tiled=True)
    own, scale = call(norm_kernel, "norm", [f32(ROWS, WIDE), f32(1, ROWS)], [trade(copies, feat)])
    oth = swap(own, "core", NC, 1)
    s, row, col = call(
        score_kernel, "scores",
        [f32(NC * ROWS, NCOL), f32(8, ROWS), f32(8, ROWS)],
        [pos, own, oth, cols, own_p, oth_p],
        [pltpu.VMEM((NC, ROWS, WIDE), jnp.bfloat16)] * 2,
    )
    row, col = call(relay_kernel, "relay", [f32(NF, 8, ROWS), f32(NZ // 2 * NYH, 8, ROWS)],
                    [row, swap(row, "core", NC, 1), col, swap(col, "zl", 2, 1)])
    rows_l = trade(row, feat)
    cols_l = trade(col, ("zh", "yh"))
    mine, theirs = call(
        grad_kernel, "gradient",
        [f32(NF, PIECE, ROWS)] * 2,
        [pos, s, own, oth, cols, own_p, oth_p, rows_l, cols_l],
        [pltpu.VMEM((NC, ROWS, NCOL), jnp.bfloat16)] * 2,
    )
    pieces = trade(mine + swap(theirs, "core", NC, 1), feat)
    loss, grad = call(last_kernel, "finish", [f32(1, 1), f32(FEAT, ROWS)], [pieces, scale])
    return loss.reshape(()), grad.T


def solution(mesh):
    fine = Mesh(mesh.devices.reshape(NZ // 2, 2, NYH, NC, NYL, NX), Z + ("yh", "core", "yl", "x"))
    rows = Z + ("yh", "core")
    return jax.shard_map(
        per_device,
        mesh=fine,
        in_specs=(P(rows, ("yl", "x")), P(rows)),
        out_specs=(P(), P(rows, ("yl", "x"))),
        check_vma=False,
    )
```

```python
import jax
import jax.numpy as jnp
from jax import lax
from jax.experimental import pallas as pl
from jax.experimental.pallas import tpu as pltpu
from jax.sharding import Mesh, PartitionSpec as P

NZ, NYH, NC, NYL, NX = 8, 4, 2, 2, 4
NF = NYL * NX
ROWS = 128
FEAT = 192
WIDE = NF * FEAT
CHUNK = ROWS // NF
NCOL = NZ * NYH * CHUNK
PIECE = FEAT + 8
BLOCK = NYH * CHUNK
HALF = BLOCK // 2
TOTAL = 8192
INV_TAU = 10.0
VMEM = pl.BlockSpec(memory_space=pltpu.VMEM)
SMEM = pl.BlockSpec(memory_space=pltpu.SMEM)
PARAMS = pltpu.CompilerParams(vmem_limit_bytes=32 * 1024 * 1024)


def f32(*shape):
    return jax.ShapeDtypeStruct(shape, jnp.float32)


def split(x):
    hi = x.astype(jnp.bfloat16)
    lo = (x - hi.astype(jnp.float32)).astype(jnp.bfloat16)
    return hi, lo


def dot3(a, b, dims):
    def one(x, y):
        return lax.dot_general(x, y, (dims, ((), ())), preferred_element_type=jnp.float32)
    return one(a[0], b[0]) + (one(a[0], b[1]) + one(a[1], b[0]))


def column(x):
    return jnp.broadcast_to(x, (ROWS, ROWS)).T[:, :1]


def pack(x):
    half = CHUNK // 2
    return jnp.concatenate([x[:, :ROWS], jnp.concatenate([x[:half, ROWS:], x[half:, ROWS:]], axis=1)], axis=0)


def unpack(x):
    tail = x[CHUNK:, :]
    rest = FEAT - ROWS
    return jnp.concatenate([x[:CHUNK, :], jnp.concatenate([tail[:, :rest], tail[:, rest:]], axis=0)], axis=1)


def chunk_kernel(view_ref, out_ref):
    x = view_ref[...].T
    for f in range(NF):
        piece = pack(x[f * CHUNK:(f + 1) * CHUNK, :])
        for y in range(NYH):
            out_ref[y * NF + f] = piece


def column_kernel(piece_ref, unit_ref):
    for y in range(NYH):
        x = jnp.concatenate([unpack(piece_ref[y * NF + f]) for f in range(NF)], axis=1)
        scale = lax.rsqrt(jnp.sum(x * x, axis=1, keepdims=True) + 1e-06)
        unit_ref[y * CHUNK:(y + 1) * CHUNK, :] = x * scale


def norm_kernel(pos_ref, piece_ref, own_ref, oth_ref, scale_ref):
    core = pos_ref[1]
    for j, out in enumerate((own_ref, oth_ref)):
        x = piece_ref[core ^ j]
        scale = lax.rsqrt(jnp.sum(x * x, axis=0, keepdims=True) + 1e-06)
        if j == 0:
            scale_ref[...] = scale
        out[...] = (x * scale).T


def tile_masks(pos_ref, half, part):
    zy, core, me = pos_ref[0], pos_ref[1], pos_ref[2]
    lane = lax.broadcasted_iota(jnp.int32, (1, NCOL), 1)
    col = ((lane // CHUNK) * NC + core) * ROWS + me * CHUNK + lane % CHUNK
    row = (zy * NC + half) * ROWS + lax.broadcasted_iota(jnp.int32, (ROWS, 1), 0)
    return col == row, col == part


def score_kernel(pos_ref, own_ref, oth_ref, ownp_ref, othp_ref, *refs):
    blocks, (s_ref, row_ref, col_ref, cols_ref, hi, lo) = refs[:-6], refs[-6:]
    core = pos_ref[1]
    z = pos_ref[0] // NYH
    for k, block in enumerate(blocks):
        whole = k < NZ - 1
        back = (k if k < NZ // 2 else k + 1) if whole else NZ // 2
        at = ((z + NZ - back) % NZ) * BLOCK + (0 if whole else (k - NZ + 1) * HALF)
        rows = BLOCK if whole else HALF
        cols_ref[pl.ds(pl.multiple_of(at, HALF), rows), :] = block[...]
    for j, ref in enumerate((own_ref, oth_ref)):
        hi[j], lo[j] = split(ref[...])
    rows = (hi[...].reshape(NC * ROWS, WIDE), lo[...].reshape(NC * ROWS, WIDE))
    step = 256
    for c in range(0, NCOL, step):
        s_ref[:, c:c + step] = INV_TAU * dot3(rows, split(cols_ref[c:c + step, :]), ((1,), (1,)))
    colsum = jnp.zeros((1, NCOL), jnp.float32)
    pos = jnp.zeros((1, ROWS), jnp.float32)
    sums = []
    for j, part in enumerate((ownp_ref, othp_ref)):
        s = s_ref[j * ROWS:(j + 1) * ROWS, :]
        diag, hit = tile_masks(pos_ref, core ^ j, part[...])
        e = jnp.where(diag, 0.0, jnp.exp(s))
        colsum = colsum + jnp.sum(e, axis=0, keepdims=True)
        lanes = e[:, :ROWS]
        hits = jnp.sum(jnp.where(hit, s, 0.0), axis=0, keepdims=True)
        for c in range(NCOL // ROWS):
            pos = pos + hits[:, c * ROWS:(c + 1) * ROWS]
            if c:
                lanes = lanes + e[:, c * ROWS:(c + 1) * ROWS]
        sums.append(jnp.sum(lanes.T, axis=0, keepdims=True))
    first = core == 0
    row = jnp.concatenate([jnp.where(first, sums[0], sums[1]), jnp.where(first, sums[1], sums[0]),
                           jnp.zeros((8 - NC, ROWS), jnp.float32)], axis=0)
    nrow = NCOL // ROWS
    col = jnp.concatenate([colsum[:, c * ROWS:(c + 1) * ROWS] for c in range(nrow)]
                          + [pos, jnp.zeros((7 - nrow, ROWS), jnp.float32)], axis=0)
    for k in range(NC * NF):
        row_ref[k] = row
    for k in range(NZ * NYH):
        col_ref[k] = col


def grad_kernel(pos_ref, s_ref, own_ref, oth_ref, cols_ref, ownp_ref, othp_ref, rows_ref, cols_l_ref, mine_ref, theirs_ref, w_hi, w_lo):
    core = pos_ref[1]
    row_l = jnp.sum(rows_ref[...], axis=0)
    col_l = jnp.sum(cols_l_ref[...], axis=0)
    nrow = NCOL // ROWS
    col_inv = jnp.concatenate([1.0 / col_l[c:c + 1, :] for c in range(nrow)], axis=1)
    loss = jnp.sum(jnp.log(col_l[:nrow, :]), axis=0, keepdims=True) - col_l[nrow:nrow + 1, :]
    projs = []
    for j, part in enumerate((ownp_ref, othp_ref)):
        s = s_ref[j * ROWS:(j + 1) * ROWS, :]
        half = core ^ j
        diag, hit = tile_masks(pos_ref, half, part[...])
        inv = column(1.0 / jnp.where(half == 0, row_l[0:1, :], row_l[1:2, :]))
        w = jnp.where(diag, 0.0, jnp.exp(s) * (inv + col_inv)) - jnp.where(hit, 2.0, 0.0)
        projs.append(jnp.sum(w * s, axis=1, keepdims=True))
        w_hi[j], w_lo[j] = split(w)
    weights = (w_hi[...].reshape(NC * ROWS, NCOL), w_lo[...].reshape(NC * ROWS, NCOL))
    step = 4 * FEAT
    tail = jnp.concatenate([loss, jnp.zeros((7, ROWS), jnp.float32)], axis=0)
    for c in range(WIDE // step):
        at = slice(c * step, (c + 1) * step)
        g = INV_TAU * dot3(weights, split(cols_ref[:, at]), ((1,), (0,)))
        for j, (units, out) in enumerate(((own_ref, mine_ref), (oth_ref, theirs_ref))):
            t = (g[j * ROWS:(j + 1) * ROWS, :] - units[:, at] * projs[j]).T
            for p in range(4):
                out[4 * c + p, :FEAT, :] = t[p * FEAT:(p + 1) * FEAT, :]
                out[4 * c + p, FEAT:, :] = tail


def last_kernel(piece_ref, scale_ref, loss_ref, grad_ref):
    total = jnp.sum(piece_ref[...], axis=0)
    loss_ref[...] = jnp.sum(total[FEAT:FEAT + 1, :], axis=1, keepdims=True) / TOTAL
    grad_ref[...] = total[:FEAT, :] * scale_ref[...]


def swap(x, axes, size, k):
    return lax.ppermute(x, axes, [(i, i ^ k) for i in range(size)])


def around(x):
    def shift(block, by):
        return lax.ppermute(block, "z", [(i, (i + by) % NZ) for i in range(NZ)])
    up, down = [x], [x]
    for _ in range(NZ // 2 - 1):
        up.append(shift(up[-1], 1))
        down.append(shift(down[-1], -1))
    return up + down[:0:-1] + [shift(up[-1][:HALF], 1), shift(down[-1][HALF:], -1)]


def trade(x, axes):
    return lax.all_to_all(x, axes, 0, 0, tiled=True)


def call(body, name, outs, args, scratch=()):
    return pl.pallas_call(
        body,
        out_shape=outs,
        in_specs=[SMEM if a.shape == (3,) else VMEM for a in args],
        out_specs=[VMEM] * len(outs),
        scratch_shapes=list(scratch),
        compiler_params=PARAMS,
        name=name,
    )(*args)


def per_device(views, partner):
    zy = lax.axis_index(("z", "yh"))
    core = lax.axis_index("core")
    me = lax.axis_index(("yl", "x"))
    pos = jnp.stack([zy, core, me]).astype(jnp.int32)
    feat = ("yl", "x")

    own_p = partner.reshape(ROWS, 1)
    oth_p = swap(partner, "core", NC, 1).reshape(ROWS, 1)
    whole = lax.all_gather(views.T, ("core", "yl", "x"), axis=0, tiled=True)
    packed = CHUNK * FEAT // ROWS
    chunks, = call(chunk_kernel, "chunks", [f32(NYH * NF, packed, ROWS)], [views.T])
    chunks = trade(chunks, ("yh", "yl", "x"))
    chunk, = call(column_kernel, "columns", [f32(BLOCK, WIDE)], [chunks])
    ring = around(chunk)
    own, oth, scale = call(norm_kernel, "norm", [f32(ROWS, WIDE)] * 2 + [f32(1, ROWS)],
                           [pos, whole.reshape(NC, WIDE, ROWS)])
    s, row, col, cols = call(
        score_kernel, "scores",
        [f32(NC * ROWS, NCOL), f32(NC * NF, 8, ROWS), f32(NZ * NYH, 8, ROWS), f32(NCOL, WIDE)],
        [pos, own, oth, own_p, oth_p, *ring],
        [pltpu.VMEM((NC, ROWS, WIDE), jnp.bfloat16)] * 2,
    )
    rows_l = trade(row, ("core", "yl", "x"))
    cols_l = trade(col, ("z", "yh"))
    mine, theirs = call(
        grad_kernel, "gradient",
        [f32(NF, PIECE, ROWS)] * 2,
        [pos, s, own, oth, cols, own_p, oth_p, rows_l, cols_l],
        [pltpu.VMEM((NC, ROWS, NCOL), jnp.bfloat16)] * 2,
    )
    pieces = trade(mine + swap(theirs, "core", NC, 1), feat)
    loss, grad = call(last_kernel, "finish", [f32(1, 1), f32(FEAT, ROWS)], [pieces, scale])
    return loss.reshape(()), grad.T


def solution(mesh):
    fine = Mesh(mesh.devices.reshape(NZ, NYH, NC, NYL, NX), ("z", "yh", "core", "yl", "x"))
    rows = ("z", "yh", "core")
    return jax.shard_map(
        per_device,
        mesh=fine,
        in_specs=(P(rows, ("yl", "x")), P(rows)),
        out_specs=(P(), P(rows, ("yl", "x"))),
        check_vma=False,
    )
```

```python
import jax
import jax.numpy as jnp
from jax import lax
from jax.experimental import pallas as pl
from jax.experimental.pallas import tpu as pltpu
from jax.sharding import Mesh, PartitionSpec as P

NZ, NYH, NC, NYL, NX = 8, 4, 2, 2, 4
NF = NYL * NX
ROWS = 128
FEAT = 192
WIDE = NF * FEAT
CHUNK = ROWS // NF
NCOL = NZ * NYH * CHUNK
PIECE = FEAT + 8
BLOCK = NYH * CHUNK
HALF = BLOCK // 2
TOTAL = 8192
INV_TAU = 10.0
VMEM = pl.BlockSpec(memory_space=pltpu.VMEM)
SMEM = pl.BlockSpec(memory_space=pltpu.SMEM)
PARAMS = pltpu.CompilerParams(vmem_limit_bytes=32 * 1024 * 1024)


def f32(*shape):
    return jax.ShapeDtypeStruct(shape, jnp.float32)


def split(x):
    hi = x.astype(jnp.bfloat16)
    lo = (x - hi.astype(jnp.float32)).astype(jnp.bfloat16)
    return hi, lo


def dot3(a, b, dims):
    def one(x, y):
        return lax.dot_general(x, y, (dims, ((), ())), preferred_element_type=jnp.float32)
    return one(a[0], b[0]) + (one(a[0], b[1]) + one(a[1], b[0]))


def column(x):
    return jnp.broadcast_to(x, (ROWS, ROWS)).T[:, :1]


def pack(x):
    half = CHUNK // 2
    return jnp.concatenate([x[:, :ROWS], jnp.concatenate([x[:half, ROWS:], x[half:, ROWS:]], axis=1)], axis=0)


def unpack(x):
    tail = x[CHUNK:, :]
    rest = FEAT - ROWS
    return jnp.concatenate([x[:CHUNK, :], jnp.concatenate([tail[:, :rest], tail[:, rest:]], axis=0)], axis=1)


def chunk_kernel(view_ref, partner_ref, out_ref, shard_ref):
    shard_ref[:FEAT, :] = view_ref[...]
    shard_ref[FEAT:, :] = jnp.broadcast_to(partner_ref[...].astype(jnp.float32), (PIECE - FEAT, ROWS))
    x = view_ref[...].T
    for f in range(NF):
        piece = pack(x[f * CHUNK:(f + 1) * CHUNK, :])
        for y in range(NYH):
            out_ref[y * NF + f] = piece


def column_kernel(piece_ref, unit_ref):
    for y in range(NYH):
        x = jnp.concatenate([unpack(piece_ref[y * NF + f]) for f in range(NF)], axis=1)
        scale = lax.rsqrt(jnp.sum(x * x, axis=1, keepdims=True) + 1e-06)
        unit_ref[y * CHUNK:(y + 1) * CHUNK, :] = x * scale


def norm_kernel(pos_ref, piece_ref, own_ref, oth_ref, scale_ref, ownp_ref, othp_ref, hi_ref, lo_ref):
    core = pos_ref[1]
    for j, (out, part) in enumerate(((own_ref, ownp_ref), (oth_ref, othp_ref))):
        x = piece_ref[core ^ j, :, :FEAT, :].reshape(WIDE, ROWS)
        scale = lax.rsqrt(jnp.sum(x * x, axis=0, keepdims=True) + 1e-06)
        if j == 0:
            scale_ref[...] = scale
        units = (x * scale).T
        out[...] = units
        part[...] = column(piece_ref[core ^ j, 0, FEAT:FEAT + 1, :]).astype(jnp.int32)
        at = slice(j * ROWS, (j + 1) * ROWS)
        hi_ref[at, :], lo_ref[at, :] = split(units)


def tile_masks(pos_ref, half, part):
    zy, core, me = pos_ref[0], pos_ref[1], pos_ref[2]
    lane = lax.broadcasted_iota(jnp.int32, (1, NCOL), 1)
    col = ((lane // CHUNK) * NC + core) * ROWS + me * CHUNK + lane % CHUNK
    row = (zy * NC + half) * ROWS + lax.broadcasted_iota(jnp.int32, (ROWS, 1), 0)
    return col == row, col == part


def score_kernel(pos_ref, hi_ref, lo_ref, ownp_ref, othp_ref, *refs):
    blocks, (s_ref, row_ref, col_ref, cols_ref) = refs[:-4], refs[-4:]
    core = pos_ref[1]
    z = pos_ref[0] // NYH
    for k, block in enumerate(blocks):
        whole = k < NZ - 1
        back = (k if k < NZ // 2 else k + 1) if whole else NZ // 2
        at = ((z + NZ - back) % NZ) * BLOCK + (0 if whole else (k - NZ + 1) * HALF)
        rows = BLOCK if whole else HALF
        cols_ref[pl.ds(pl.multiple_of(at, HALF), rows), :] = block[...]
    rows = (hi_ref[...], lo_ref[...])
    step = 256
    for c in range(0, NCOL, step):
        s_ref[:, c:c + step] = INV_TAU * dot3(rows, split(cols_ref[c:c + step, :]), ((1,), (1,)))
    colsum = jnp.zeros((1, NCOL), jnp.float32)
    pos = jnp.zeros((1, ROWS), jnp.float32)
    sums = []
    for j, part in enumerate((ownp_ref, othp_ref)):
        s = s_ref[j * ROWS:(j + 1) * ROWS, :]
        diag, hit = tile_masks(pos_ref, core ^ j, part[...])
        e = jnp.where(diag, 0.0, jnp.exp(s))
        colsum = colsum + jnp.sum(e, axis=0, keepdims=True)
        lanes = e[:, :ROWS]
        hits = jnp.sum(jnp.where(hit, s, 0.0), axis=0, keepdims=True)
        for c in range(NCOL // ROWS):
            pos = pos + hits[:, c * ROWS:(c + 1) * ROWS]
            if c:
                lanes = lanes + e[:, c * ROWS:(c + 1) * ROWS]
        sums.append(jnp.sum(lanes.T, axis=0, keepdims=True))
    first = core == 0
    row = jnp.concatenate([jnp.where(first, sums[0], sums[1]), jnp.where(first, sums[1], sums[0]),
                           jnp.zeros((8 - NC, ROWS), jnp.float32)], axis=0)
    nrow = NCOL // ROWS
    col = jnp.concatenate([colsum[:, c * ROWS:(c + 1) * ROWS] for c in range(nrow)]
                          + [pos, jnp.zeros((7 - nrow, ROWS), jnp.float32)], axis=0)
    for k in range(NC * NF):
        row_ref[k] = row
    for k in range(NZ * NYH):
        col_ref[k] = col


def grad_kernel(pos_ref, s_ref, own_ref, oth_ref, cols_ref, ownp_ref, othp_ref, rows_ref, cols_l_ref, mine_ref, theirs_ref, w_hi, w_lo):
    core = pos_ref[1]
    row_l = jnp.sum(rows_ref[...], axis=0)
    col_l = jnp.sum(cols_l_ref[...], axis=0)
    nrow = NCOL // ROWS
    col_inv = jnp.concatenate([1.0 / col_l[c:c + 1, :] for c in range(nrow)], axis=1)
    loss = jnp.sum(jnp.log(col_l[:nrow, :]), axis=0, keepdims=True) - col_l[nrow:nrow + 1, :]
    projs = []
    for j, part in enumerate((ownp_ref, othp_ref)):
        s = s_ref[j * ROWS:(j + 1) * ROWS, :]
        half = core ^ j
        diag, hit = tile_masks(pos_ref, half, part[...])
        inv = column(1.0 / jnp.where(half == 0, row_l[0:1, :], row_l[1:2, :]))
        w = jnp.where(diag, 0.0, jnp.exp(s) * (inv + col_inv)) - jnp.where(hit, 2.0, 0.0)
        projs.append(jnp.sum(w * s, axis=1, keepdims=True))
        w_hi[j], w_lo[j] = split(w)
    weights = (w_hi[...].reshape(NC * ROWS, NCOL), w_lo[...].reshape(NC * ROWS, NCOL))
    step = 4 * FEAT
    tail = jnp.concatenate([loss, jnp.zeros((7, ROWS), jnp.float32)], axis=0)
    for c in range(WIDE // step):
        at = slice(c * step, (c + 1) * step)
        g = INV_TAU * dot3(weights, split(cols_ref[:, at]), ((1,), (0,)))
        for j, (units, out) in enumerate(((own_ref, mine_ref), (oth_ref, theirs_ref))):
            t = (g[j * ROWS:(j + 1) * ROWS, :] - units[:, at] * projs[j]).T
            for p in range(4):
                out[4 * c + p, :FEAT, :] = t[p * FEAT:(p + 1) * FEAT, :]
                out[4 * c + p, FEAT:, :] = tail


def last_kernel(piece_ref, scale_ref, loss_ref, grad_ref):
    total = jnp.sum(piece_ref[...], axis=0)
    loss_ref[...] = jnp.sum(total[FEAT:FEAT + 1, :], axis=1, keepdims=True) / TOTAL
    grad_ref[...] = total[:FEAT, :] * scale_ref[...]


def swap(x, axes, size, k):
    return lax.ppermute(x, axes, [(i, i ^ k) for i in range(size)])


def around(x):
    def shift(block, by):
        return lax.ppermute(block, "z", [(i, (i + by) % NZ) for i in range(NZ)])
    up, down = [x], [x]
    for _ in range(NZ // 2 - 1):
        up.append(shift(up[-1], 1))
        down.append(shift(down[-1], -1))
    return up + down[:0:-1] + [shift(up[-1][:HALF], 1), shift(down[-1][HALF:], -1)]


def trade(x, axes):
    return lax.all_to_all(x, axes, 0, 0, tiled=True)


def call(body, name, outs, args, scratch=()):
    return pl.pallas_call(
        body,
        out_shape=outs,
        in_specs=[SMEM if a.shape == (3,) else VMEM for a in args],
        out_specs=[VMEM] * len(outs),
        scratch_shapes=list(scratch),
        compiler_params=PARAMS,
        name=name,
    )(*args)


def per_device(views, partner):
    zy = lax.axis_index(("z", "yh"))
    core = lax.axis_index("core")
    me = lax.axis_index(("yl", "x"))
    pos = jnp.stack([zy, core, me]).astype(jnp.int32)
    feat = ("yl", "x")

    packed = CHUNK * FEAT // ROWS
    chunks, shard = call(chunk_kernel, "chunks", [f32(NYH * NF, packed, ROWS), f32(PIECE, ROWS)],
                         [views.T, partner.reshape(1, ROWS)])
    whole = lax.all_gather(shard, ("core", "yl", "x"), axis=0, tiled=True)
    chunks = trade(chunks, ("yh", "yl", "x"))
    chunk, = call(column_kernel, "columns", [f32(BLOCK, WIDE)], [chunks])
    ring = around(chunk)
    ids, bf16 = jax.ShapeDtypeStruct((ROWS, 1), jnp.int32), jax.ShapeDtypeStruct((NC * ROWS, WIDE), jnp.bfloat16)
    own, oth, scale, own_p, oth_p, hi, lo = call(
        norm_kernel, "norm",
        [f32(ROWS, WIDE)] * 2 + [f32(1, ROWS), ids, ids, bf16, bf16],
        [pos, whole.reshape(NC, NF, PIECE, ROWS)],
    )
    s, row, col, cols = call(
        score_kernel, "scores",
        [f32(NC * ROWS, NCOL), f32(NC * NF, 8, ROWS), f32(NZ * NYH, 8, ROWS), f32(NCOL, WIDE)],
        [pos, hi, lo, own_p, oth_p, *ring],
    )
    rows_l = trade(row, ("core", "yl", "x"))
    cols_l = trade(col, ("z", "yh"))
    mine, theirs = call(
        grad_kernel, "gradient",
        [f32(NF, PIECE, ROWS)] * 2,
        [pos, s, own, oth, cols, own_p, oth_p, rows_l, cols_l],
        [pltpu.VMEM((NC, ROWS, NCOL), jnp.bfloat16)] * 2,
    )
    pieces = trade(mine + swap(theirs, "core", NC, 1), feat)
    loss, grad = call(last_kernel, "finish", [f32(1, 1), f32(FEAT, ROWS)], [pieces, scale])
    return loss.reshape(()), grad.T


def solution(mesh):
    fine = Mesh(mesh.devices.reshape(NZ, NYH, NC, NYL, NX), ("z", "yh", "core", "yl", "x"))
    rows = ("z", "yh", "core")
    return jax.shard_map(
        per_device,
        mesh=fine,
        in_specs=(P(rows, ("yl", "x")), P(rows)),
        out_specs=(P(), P(rows, ("yl", "x"))),
        check_vma=False,
    )
```

```python
import jax
import jax.numpy as jnp
from jax import lax
from jax.experimental import pallas as pl
from jax.experimental.pallas import tpu as pltpu
from jax.sharding import Mesh, PartitionSpec as P

NZ, NYH, NC, NYL, NX = 8, 4, 2, 2, 4
NF = NYL * NX
ROWS = 128
FEAT = 192
WIDE = NF * FEAT
CHUNK = ROWS // NF
NCOL = NZ * NYH * CHUNK
PIECE = FEAT + 8
BLOCK = NYH * CHUNK
HALF = BLOCK // 2
TOTAL = 8192
INV_TAU = 10.0
VMEM = pl.BlockSpec(memory_space=pltpu.VMEM)
SMEM = pl.BlockSpec(memory_space=pltpu.SMEM)
PARAMS = pltpu.CompilerParams(vmem_limit_bytes=32 * 1024 * 1024)


def f32(*shape):
    return jax.ShapeDtypeStruct(shape, jnp.float32)


def split(x):
    hi = x.astype(jnp.bfloat16)
    lo = (x - hi.astype(jnp.float32)).astype(jnp.bfloat16)
    return hi, lo


def dot3(a, b, dims):
    def one(x, y):
        return lax.dot_general(x, y, (dims, ((), ())), preferred_element_type=jnp.float32)
    return one(a[0], b[0]) + (one(a[0], b[1]) + one(a[1], b[0]))


def column(x):
    return jnp.broadcast_to(x, (ROWS, ROWS)).T[:, :1]


def pack(x):
    half = CHUNK // 2
    return jnp.concatenate([x[:, :ROWS], jnp.concatenate([x[:half, ROWS:], x[half:, ROWS:]], axis=1)], axis=0)


def unpack(x):
    tail = x[CHUNK:, :]
    rest = FEAT - ROWS
    return jnp.concatenate([x[:CHUNK, :], jnp.concatenate([tail[:, :rest], tail[:, rest:]], axis=0)], axis=1)


def chunk_kernel(view_ref, out_ref, copy_ref):
    copy_ref[...] = view_ref[...]
    x = view_ref[...].T
    for f in range(NF):
        piece = pack(x[f * CHUNK:(f + 1) * CHUNK, :])
        for y in range(NYH):
            out_ref[y * NF + f] = piece


def column_kernel(piece_ref, view_ref, partner_ref, unit_ref, shard_ref):
    shard_ref[:FEAT, :] = view_ref[...]
    shard_ref[FEAT:, :] = jnp.broadcast_to(partner_ref[...].astype(jnp.float32), (PIECE - FEAT, ROWS))
    for y in range(NYH):
        x = jnp.concatenate([unpack(piece_ref[y * NF + f]) for f in range(NF)], axis=1)
        scale = lax.rsqrt(jnp.sum(x * x, axis=1, keepdims=True) + 1e-06)
        unit_ref[y * CHUNK:(y + 1) * CHUNK, :] = x * scale


def norm_kernel(pos_ref, piece_ref, own_ref, oth_ref, scale_ref, ownp_ref, othp_ref, hi_ref, lo_ref):
    core = pos_ref[1]
    for j, (out, part) in enumerate(((own_ref, ownp_ref), (oth_ref, othp_ref))):
        x = piece_ref[core ^ j, :, :FEAT, :].reshape(WIDE, ROWS)
        scale = lax.rsqrt(jnp.sum(x * x, axis=0, keepdims=True) + 1e-06)
        if j == 0:
            scale_ref[...] = scale
        units = (x * scale).T
        out[...] = units
        part[...] = column(piece_ref[core ^ j, 0, FEAT:FEAT + 1, :]).astype(jnp.int32)
        at = slice(j * ROWS, (j + 1) * ROWS)
        hi_ref[at, :], lo_ref[at, :] = split(units)


def tile_masks(pos_ref, half, part):
    zy, core, me = pos_ref[0], pos_ref[1], pos_ref[2]
    lane = lax.broadcasted_iota(jnp.int32, (1, NCOL), 1)
    col = ((lane // CHUNK) * NC + core) * ROWS + me * CHUNK + lane % CHUNK
    row = (zy * NC + half) * ROWS + lax.broadcasted_iota(jnp.int32, (ROWS, 1), 0)
    return col == row, col == part


def score_kernel(pos_ref, hi_ref, lo_ref, ownp_ref, othp_ref, *refs):
    blocks, (s_ref, row_ref, col_ref, cols_ref) = refs[:-4], refs[-4:]
    core = pos_ref[1]
    z = pos_ref[0] // NYH
    for k, block in enumerate(blocks):
        whole = k < NZ - 1
        ahead = (k if k < NZ // 2 else NZ // 2 - 1 - k) if whole else NZ // 2
        at = ((z + NZ + ahead * (1 - 2 * (z % 2))) % NZ) * BLOCK + (0 if whole else (k - NZ + 1) * HALF)
        rows = BLOCK if whole else HALF
        cols_ref[pl.ds(pl.multiple_of(at, HALF), rows), :] = block[...]
    rows = (hi_ref[...], lo_ref[...])
    step = 256
    for c in range(0, NCOL, step):
        s_ref[:, c:c + step] = INV_TAU * dot3(rows, split(cols_ref[c:c + step, :]), ((1,), (1,)))
    colsum = jnp.zeros((1, NCOL), jnp.float32)
    pos = jnp.zeros((1, ROWS), jnp.float32)
    sums = []
    for j, part in enumerate((ownp_ref, othp_ref)):
        s = s_ref[j * ROWS:(j + 1) * ROWS, :]
        diag, hit = tile_masks(pos_ref, core ^ j, part[...])
        e = jnp.where(diag, 0.0, jnp.exp(s))
        colsum = colsum + jnp.sum(e, axis=0, keepdims=True)
        lanes = e[:, :ROWS]
        hits = jnp.sum(jnp.where(hit, s, 0.0), axis=0, keepdims=True)
        for c in range(NCOL // ROWS):
            pos = pos + hits[:, c * ROWS:(c + 1) * ROWS]
            if c:
                lanes = lanes + e[:, c * ROWS:(c + 1) * ROWS]
        sums.append(jnp.sum(lanes.T, axis=0, keepdims=True))
    first = core == 0
    row = jnp.concatenate([jnp.where(first, sums[0], sums[1]), jnp.where(first, sums[1], sums[0]),
                           jnp.zeros((8 - NC, ROWS), jnp.float32)], axis=0)
    nrow = NCOL // ROWS
    col = jnp.concatenate([colsum[:, c * ROWS:(c + 1) * ROWS] for c in range(nrow)]
                          + [pos, jnp.zeros((7 - nrow, ROWS), jnp.float32)], axis=0)
    for k in range(NC * NF):
        row_ref[k] = row
    for k in range(NZ * NYH):
        col_ref[k] = col


def grad_kernel(pos_ref, s_ref, own_ref, oth_ref, cols_ref, ownp_ref, othp_ref, rows_ref, cols_l_ref, mine_ref, theirs_ref, w_hi, w_lo):
    core = pos_ref[1]
    row_l = jnp.sum(rows_ref[...], axis=0)
    col_l = jnp.sum(cols_l_ref[...], axis=0)
    nrow = NCOL // ROWS
    col_inv = jnp.concatenate([1.0 / col_l[c:c + 1, :] for c in range(nrow)], axis=1)
    loss = jnp.sum(jnp.log(col_l[:nrow, :]), axis=0, keepdims=True) - col_l[nrow:nrow + 1, :]
    projs = []
    for j, part in enumerate((ownp_ref, othp_ref)):
        s = s_ref[j * ROWS:(j + 1) * ROWS, :]
        half = core ^ j
        diag, hit = tile_masks(pos_ref, half, part[...])
        inv = column(1.0 / jnp.where(half == 0, row_l[0:1, :], row_l[1:2, :]))
        w = jnp.where(diag, 0.0, jnp.exp(s) * (inv + col_inv)) - jnp.where(hit, 2.0, 0.0)
        projs.append(jnp.sum(w * s, axis=1, keepdims=True))
        w_hi[j], w_lo[j] = split(w)
    weights = (w_hi[...].reshape(NC * ROWS, NCOL), w_lo[...].reshape(NC * ROWS, NCOL))
    step = 4 * FEAT
    tail = jnp.concatenate([loss, jnp.zeros((7, ROWS), jnp.float32)], axis=0)
    for c in range(WIDE // step):
        at = slice(c * step, (c + 1) * step)
        g = INV_TAU * dot3(weights, split(cols_ref[:, at]), ((1,), (0,)))
        for j, (units, out) in enumerate(((own_ref, mine_ref), (oth_ref, theirs_ref))):
            t = (g[j * ROWS:(j + 1) * ROWS, :] - units[:, at] * projs[j]).T
            for p in range(4):
                out[4 * c + p, :FEAT, :] = t[p * FEAT:(p + 1) * FEAT, :]
                out[4 * c + p, FEAT:, :] = tail


def last_kernel(piece_ref, scale_ref, loss_ref, grad_ref):
    total = jnp.sum(piece_ref[...], axis=0)
    loss_ref[...] = jnp.sum(total[FEAT:FEAT + 1, :], axis=1, keepdims=True) / TOTAL
    grad_ref[...] = total[:FEAT, :] * scale_ref[...]


def swap(x, axes, size, k):
    return lax.ppermute(x, axes, [(i, i ^ k) for i in range(size)])


def around(x):
    pair = [(i, i ^ 1) for i in range(NZ)]
    between = [(i, ((i - 1) ^ 1) + 1 & NZ - 1) for i in range(NZ)]
    a, b = [x], [x]
    for _ in range(NZ // 2 - 1):
        got = lax.ppermute(b[-1], "z", pair), lax.ppermute(a[-1], "z", between)
        a.append(got[0])
        b.append(got[1])
    last = lax.ppermute(b[-1][:HALF], "z", pair), lax.ppermute(a[-1][HALF:], "z", between)
    return a + b[1:] + list(last)


def trade(x, axes):
    return lax.all_to_all(x, axes, 0, 0, tiled=True)


def call(body, name, outs, args, scratch=()):
    return pl.pallas_call(
        body,
        out_shape=outs,
        in_specs=[SMEM if a.shape == (3,) else VMEM for a in args],
        out_specs=[VMEM] * len(outs),
        scratch_shapes=list(scratch),
        compiler_params=PARAMS,
        name=name,
    )(*args)


def per_device(views, partner):
    zy = lax.axis_index(("z", "yh"))
    core = lax.axis_index("core")
    me = lax.axis_index(("yl", "x"))
    pos = jnp.stack([zy, core, me]).astype(jnp.int32)
    feat = ("yl", "x")

    packed = CHUNK * FEAT // ROWS
    chunks, copy = call(chunk_kernel, "chunks", [f32(NYH * NF, packed, ROWS), f32(FEAT, ROWS)], [views.T])
    chunk, shard = call(column_kernel, "columns", [f32(BLOCK, WIDE), f32(PIECE, ROWS)],
                        [trade(chunks, ("yh", "yl", "x")), copy, partner.reshape(1, ROWS)])
    whole = lax.all_gather(shard, ("core", "yl", "x"), axis=0, tiled=True)
    ring = around(chunk)
    ids, bf16 = jax.ShapeDtypeStruct((ROWS, 1), jnp.int32), jax.ShapeDtypeStruct((NC * ROWS, WIDE), jnp.bfloat16)
    own, oth, scale, own_p, oth_p, hi, lo = call(
        norm_kernel, "norm",
        [f32(ROWS, WIDE)] * 2 + [f32(1, ROWS), ids, ids, bf16, bf16],
        [pos, whole.reshape(NC, NF, PIECE, ROWS)],
    )
    s, row, col, cols = call(
        score_kernel, "scores",
        [f32(NC * ROWS, NCOL), f32(NC * NF, 8, ROWS), f32(NZ * NYH, 8, ROWS), f32(NCOL, WIDE)],
        [pos, hi, lo, own_p, oth_p, *ring],
    )
    rows_l = trade(row, ("core", "yl", "x"))
    cols_l = trade(col, ("z", "yh"))
    mine, theirs = call(
        grad_kernel, "gradient",
        [f32(NF, PIECE, ROWS)] * 2,
        [pos, s, own, oth, cols, own_p, oth_p, rows_l, cols_l],
        [pltpu.VMEM((NC, ROWS, NCOL), jnp.bfloat16)] * 2,
    )
    pieces = trade(mine + swap(theirs, "core", NC, 1), feat)
    loss, grad = call(last_kernel, "finish", [f32(1, 1), f32(FEAT, ROWS)], [pieces, scale])
    return loss.reshape(()), grad.T


def solution(mesh):
    fine = Mesh(mesh.devices.reshape(NZ, NYH, NC, NYL, NX), ("z", "yh", "core", "yl", "x"))
    rows = ("z", "yh", "core")
    return jax.shard_map(
        per_device,
        mesh=fine,
        in_specs=(P(rows, ("yl", "x")), P(rows)),
        out_specs=(P(), P(rows, ("yl", "x"))),
        check_vma=False,
    )
```

```python
import jax
import jax.numpy as jnp
from jax import lax
from jax.experimental import pallas as pl
from jax.experimental.pallas import tpu as pltpu
from jax.sharding import Mesh, PartitionSpec as P

NZ, NYH, NC, NYL, NX = 8, 4, 2, 2, 4
NF = NYL * NX
ROWS = 128
FEAT = 192
WIDE = NF * FEAT
CHUNK = ROWS // NF
NCOL = NZ * NYH * CHUNK
PIECE = FEAT + 8
BLOCK = NYH * CHUNK
HALF = BLOCK // 2
TOTAL = 8192
INV_TAU = 10.0
VMEM = pl.BlockSpec(memory_space=pltpu.VMEM)
SMEM = pl.BlockSpec(memory_space=pltpu.SMEM)
PARAMS = pltpu.CompilerParams(vmem_limit_bytes=32 * 1024 * 1024)


def f32(*shape):
    return jax.ShapeDtypeStruct(shape, jnp.float32)


def split(x):
    hi = x.astype(jnp.bfloat16)
    lo = (x - hi.astype(jnp.float32)).astype(jnp.bfloat16)
    return hi, lo


def dot3(a, b, dims):
    def one(x, y):
        return lax.dot_general(x, y, (dims, ((), ())), preferred_element_type=jnp.float32)
    return one(a[0], b[0]) + (one(a[0], b[1]) + one(a[1], b[0]))


def column(x):
    return jnp.broadcast_to(x, (ROWS, ROWS)).T[:, :1]


def pack(x):
    half = CHUNK // 2
    return jnp.concatenate([x[:, :ROWS], jnp.concatenate([x[:half, ROWS:], x[half:, ROWS:]], axis=1)], axis=0)


def unpack(x):
    tail = x[CHUNK:, :]
    rest = FEAT - ROWS
    return jnp.concatenate([x[:CHUNK, :], jnp.concatenate([tail[:, :rest], tail[:, rest:]], axis=0)], axis=1)


def chunk_kernel(view_ref, out_ref, copy_ref):
    copy_ref[...] = view_ref[...]
    x = view_ref[...].T
    for f in range(NF):
        piece = pack(x[f * CHUNK:(f + 1) * CHUNK, :])
        for y in range(NYH):
            out_ref[y * NF + f] = piece


def column_kernel(piece_ref, view_ref, partner_ref, unit_ref, shard_ref):
    shard_ref[:FEAT, :] = view_ref[...]
    shard_ref[FEAT:, :] = jnp.broadcast_to(partner_ref[...].astype(jnp.float32), (PIECE - FEAT, ROWS))
    for y in range(NYH):
        x = jnp.concatenate([unpack(piece_ref[y * NF + f]) for f in range(NF)], axis=1)
        scale = lax.rsqrt(jnp.sum(x * x, axis=1, keepdims=True) + 1e-06)
        unit_ref[y * CHUNK:(y + 1) * CHUNK, :] = x * scale


def norm_kernel(pos_ref, piece_ref, scale_ref, ownp_ref, othp_ref, hi_ref, lo_ref):
    core = pos_ref[1]
    for j, part in enumerate((ownp_ref, othp_ref)):
        x = piece_ref[core ^ j, :, :FEAT, :].reshape(WIDE, ROWS)
        scale = lax.rsqrt(jnp.sum(x * x, axis=0, keepdims=True) + 1e-06)
        if j == 0:
            scale_ref[...] = scale
        units = (x * scale).T
        part[...] = column(piece_ref[core ^ j, 0, FEAT:FEAT + 1, :]).astype(jnp.int32)
        at = slice(j * ROWS, (j + 1) * ROWS)
        hi_ref[at, :], lo_ref[at, :] = split(units)


def tile_masks(pos_ref, half, part):
    zy, core, me = pos_ref[0], pos_ref[1], pos_ref[2]
    lane = lax.broadcasted_iota(jnp.int32, (1, NCOL), 1)
    col = ((lane // CHUNK) * NC + core) * ROWS + me * CHUNK + lane % CHUNK
    row = (zy * NC + half) * ROWS + lax.broadcasted_iota(jnp.int32, (ROWS, 1), 0)
    return col == row, col == part


def place(z, ahead):
    return (z + NZ + ahead * (1 - 2 * (z % 2))) % NZ * BLOCK


def gather_blocks(z, blocks, cols_ref):
    for k, block in enumerate(blocks):
        ahead = k if k < NZ // 2 else NZ // 2 - 1 - k
        cols_ref[pl.ds(pl.multiple_of(place(z, ahead), BLOCK), BLOCK), :] = block[...]


def early_kernel(pos_ref, hi_ref, lo_ref, *refs):
    blocks, (s_ref, cols) = refs[:-2], refs[-2:]
    z = pos_ref[0] // NYH
    gather_blocks(z, blocks, cols)
    late = pl.multiple_of(place(z, NZ // 2), BLOCK)
    cols[pl.ds(late, BLOCK), :] = jnp.zeros((BLOCK, WIDE), jnp.float32)
    rows = (hi_ref[...], lo_ref[...])
    step = 256
    for c in range(0, NCOL, step):
        s_ref[:, c:c + step] = INV_TAU * dot3(rows, split(cols[c:c + step, :]), ((1,), (1,)))


def score_kernel(pos_ref, hi_ref, lo_ref, ownp_ref, othp_ref, early_ref, *refs):
    blocks, (s_ref, row_ref, col_ref, cols_ref) = refs[:-4], refs[-4:]
    core = pos_ref[1]
    z = pos_ref[0] // NYH
    gather_blocks(z, blocks[:-2], cols_ref)
    late = place(z, NZ // 2)
    for k, half in enumerate(blocks[-2:]):
        cols_ref[pl.ds(pl.multiple_of(late + k * HALF, HALF), HALF), :] = half[...]
    s_ref[...] = early_ref[...]
    at = pl.ds(pl.multiple_of(late // ROWS * ROWS, ROWS), ROWS)
    s_ref[:, at] = INV_TAU * dot3((hi_ref[...], lo_ref[...]), split(cols_ref[at, :]), ((1,), (1,)))
    colsum = jnp.zeros((1, NCOL), jnp.float32)
    pos = jnp.zeros((1, ROWS), jnp.float32)
    sums = []
    for j, part in enumerate((ownp_ref, othp_ref)):
        s = s_ref[j * ROWS:(j + 1) * ROWS, :]
        diag, hit = tile_masks(pos_ref, core ^ j, part[...])
        e = jnp.where(diag, 0.0, jnp.exp(s))
        colsum = colsum + jnp.sum(e, axis=0, keepdims=True)
        lanes = e[:, :ROWS]
        hits = jnp.sum(jnp.where(hit, s, 0.0), axis=0, keepdims=True)
        for c in range(NCOL // ROWS):
            pos = pos + hits[:, c * ROWS:(c + 1) * ROWS]
            if c:
                lanes = lanes + e[:, c * ROWS:(c + 1) * ROWS]
        sums.append(jnp.sum(lanes.T, axis=0, keepdims=True))
    first = core == 0
    row = jnp.concatenate([jnp.where(first, sums[0], sums[1]), jnp.where(first, sums[1], sums[0]),
                           jnp.zeros((8 - NC, ROWS), jnp.float32)], axis=0)
    nrow = NCOL // ROWS
    col = jnp.concatenate([colsum[:, c * ROWS:(c + 1) * ROWS] for c in range(nrow)]
                          + [pos, jnp.zeros((7 - nrow, ROWS), jnp.float32)], axis=0)
    for k in range(NC * NF):
        row_ref[k] = row
    for k in range(NZ * NYH):
        col_ref[k] = col


def grad_kernel(pos_ref, s_ref, cols_ref, ownp_ref, othp_ref, rows_ref, cols_l_ref, mine_ref, theirs_ref, w_hi, w_lo):
    core = pos_ref[1]
    row_l = jnp.sum(rows_ref[...], axis=0)
    col_l = jnp.sum(cols_l_ref[...], axis=0)
    nrow = NCOL // ROWS
    col_inv = jnp.concatenate([1.0 / col_l[c:c + 1, :] for c in range(nrow)], axis=1)
    loss = jnp.sum(jnp.log(col_l[:nrow, :]), axis=0, keepdims=True) - col_l[nrow:nrow + 1, :]
    projs = []
    for j, part in enumerate((ownp_ref, othp_ref)):
        s = s_ref[j * ROWS:(j + 1) * ROWS, :]
        half = core ^ j
        diag, hit = tile_masks(pos_ref, half, part[...])
        inv = column(1.0 / jnp.where(half == 0, row_l[0:1, :], row_l[1:2, :]))
        w = jnp.where(diag, 0.0, jnp.exp(s) * (inv + col_inv)) - jnp.where(hit, 2.0, 0.0)
        ws = w * s
        lanes = sum(ws[:, c * ROWS:(c + 1) * ROWS] for c in range(NCOL // ROWS))
        projs.append(jnp.sum(lanes.T, axis=0, keepdims=True))
        w_hi[j], w_lo[j] = split(w)
    weights = (w_hi[...].reshape(NC * ROWS, NCOL), w_lo[...].reshape(NC * ROWS, NCOL))
    step = 4 * FEAT
    tails = [jnp.concatenate([loss, proj, jnp.zeros((6, ROWS), jnp.float32)], axis=0) for proj in projs]
    for c in range(WIDE // step):
        at = slice(c * step, (c + 1) * step)
        g = INV_TAU * dot3(weights, split(cols_ref[:, at]), ((1,), (0,)))
        for j, out in enumerate((mine_ref, theirs_ref)):
            t = g[j * ROWS:(j + 1) * ROWS, :].T
            for p in range(4):
                out[4 * c + p, :FEAT, :] = t[p * FEAT:(p + 1) * FEAT, :]
                out[4 * c + p, FEAT:, :] = tails[j]


def last_kernel(piece_ref, scale_ref, view_ref, loss_ref, grad_ref):
    total = jnp.sum(piece_ref[...], axis=0)
    loss_ref[...] = jnp.sum(total[FEAT:FEAT + 1, :], axis=1, keepdims=True) / TOTAL
    scale = scale_ref[...]
    grad_ref[...] = (total[:FEAT, :] - view_ref[...] * scale * total[FEAT + 1:FEAT + 2, :]) * scale


def swap(x, axes, size, k):
    return lax.ppermute(x, axes, [(i, i ^ k) for i in range(size)])


def around(x):
    pair = [(i, i ^ 1) for i in range(NZ)]
    between = [(i, ((i - 1) ^ 1) + 1 & NZ - 1) for i in range(NZ)]
    a, b = [x], [x]
    for _ in range(NZ // 2 - 1):
        got = lax.ppermute(b[-1], "z", pair), lax.ppermute(a[-1], "z", between)
        a.append(got[0])
        b.append(got[1])
    last = lax.ppermute(b[-1][:HALF], "z", pair), lax.ppermute(a[-1][HALF:], "z", between)
    return a + b[1:] + list(last)


def trade(x, axes):
    return lax.all_to_all(x, axes, 0, 0, tiled=True)


def call(body, name, outs, args, scratch=()):
    return pl.pallas_call(
        body,
        out_shape=outs,
        in_specs=[SMEM if a.shape == (3,) else VMEM for a in args],
        out_specs=[VMEM] * len(outs),
        scratch_shapes=list(scratch),
        compiler_params=PARAMS,
        name=name,
    )(*args)


def per_device(views, partner):
    zy = lax.axis_index(("z", "yh"))
    core = lax.axis_index("core")
    me = lax.axis_index(("yl", "x"))
    pos = jnp.stack([zy, core, me]).astype(jnp.int32)
    feat = ("yl", "x")

    packed = CHUNK * FEAT // ROWS
    chunks, copy = call(chunk_kernel, "chunks", [f32(NYH * NF, packed, ROWS), f32(FEAT, ROWS)], [views.T])
    chunk, shard = call(column_kernel, "columns", [f32(BLOCK, WIDE), f32(PIECE, ROWS)],
                        [trade(chunks, ("yh", "yl", "x")), copy, partner.reshape(1, ROWS)])
    whole = lax.all_gather(shard, ("core", "yl", "x"), axis=0, tiled=True)
    ring = around(chunk)
    ids, bf16 = jax.ShapeDtypeStruct((ROWS, 1), jnp.int32), jax.ShapeDtypeStruct((NC * ROWS, WIDE), jnp.bfloat16)
    scale, own_p, oth_p, hi, lo = call(
        norm_kernel, "norm",
        [f32(1, ROWS), ids, ids, bf16, bf16],
        [pos, whole.reshape(NC, NF, PIECE, ROWS)],
    )
    early, = call(early_kernel, "early", [f32(NC * ROWS, NCOL)], [pos, hi, lo, *ring[:-2]],
                  [pltpu.VMEM((NCOL, WIDE), jnp.float32)])
    s, row, col, cols = call(
        score_kernel, "scores",
        [f32(NC * ROWS, NCOL), f32(NC * NF, 8, ROWS), f32(NZ * NYH, 8, ROWS), f32(NCOL, WIDE)],
        [pos, hi, lo, own_p, oth_p, early, *ring],
    )
    rows_l = trade(row, ("core", "yl", "x"))
    cols_l = trade(col, ("z", "yh"))
    mine, theirs = call(
        grad_kernel, "gradient",
        [f32(NF, PIECE, ROWS)] * 2,
        [pos, s, cols, own_p, oth_p, rows_l, cols_l],
        [pltpu.VMEM((NC, ROWS, NCOL), jnp.bfloat16)] * 2,
    )
    pieces = trade(mine + swap(theirs, "core", NC, 1), feat)
    loss, grad = call(last_kernel, "finish", [f32(1, 1), f32(FEAT, ROWS)], [pieces, scale, copy])
    return loss.reshape(()), grad.T


def solution(mesh):
    fine = Mesh(mesh.devices.reshape(NZ, NYH, NC, NYL, NX), ("z", "yh", "core", "yl", "x"))
    rows = ("z", "yh", "core")
    return jax.shard_map(
        per_device,
        mesh=fine,
        in_specs=(P(rows, ("yl", "x")), P(rows)),
        out_specs=(P(), P(rows, ("yl", "x"))),
        check_vma=False,
    )
```

```python
import jax
import jax.numpy as jnp
from jax import lax
from jax.experimental import pallas as pl
from jax.experimental.pallas import tpu as pltpu
from jax.sharding import Mesh, PartitionSpec as P

NZ, NYH, NC, NYL, NX = 8, 4, 2, 2, 4
NF = NYL * NX
ROWS = 128
FEAT = 192
WIDE = NF * FEAT
CHUNK = ROWS // NF
NCOL = NZ * NYH * CHUNK
PIECE = FEAT + 8
BLOCK = NYH * CHUNK
TOTAL = 8192
INV_TAU = 10.0
VMEM = pl.BlockSpec(memory_space=pltpu.VMEM)
SMEM = pl.BlockSpec(memory_space=pltpu.SMEM)
HBM = pl.BlockSpec(memory_space=pltpu.HBM)


def f32(*shape):
    return jax.ShapeDtypeStruct(shape, jnp.float32)


def split(x):
    hi = x.astype(jnp.bfloat16)
    lo = (x - hi.astype(jnp.float32)).astype(jnp.bfloat16)
    return hi, lo


def dot3(a, b, dims):
    def one(x, y):
        return lax.dot_general(x, y, (dims, ((), ())), preferred_element_type=jnp.float32)
    return one(a[0], b[0]) + (one(a[0], b[1]) + one(a[1], b[0]))


def column(x):
    return jnp.broadcast_to(x, (ROWS, ROWS)).T[:, :1]


def pack(x):
    half = CHUNK // 2
    return jnp.concatenate([x[:, :ROWS], jnp.concatenate([x[:half, ROWS:], x[half:, ROWS:]], axis=1)], axis=0)


def unpack(x):
    tail = x[CHUNK:, :]
    rest = FEAT - ROWS
    return jnp.concatenate([x[:CHUNK, :], jnp.concatenate([tail[:, :rest], tail[:, rest:]], axis=0)], axis=1)


def chunk_kernel(view_ref, out_ref, copy_ref):
    copy_ref[...] = view_ref[...]
    x = view_ref[...].T
    for f in range(NF):
        piece = pack(x[f * CHUNK:(f + 1) * CHUNK, :])
        for y in range(NYH):
            out_ref[y * NF + f] = piece


def column_kernel(piece_ref, view_ref, unit_ref, copies_ref):
    for f in range(NF):
        copies_ref[f] = view_ref[...]
    for y in range(NYH):
        x = jnp.concatenate([unpack(piece_ref[y * NF + f]) for f in range(NF)], axis=1)
        scale = lax.rsqrt(jnp.sum(x * x, axis=1, keepdims=True) + 1e-06)
        unit_ref[y * CHUNK:(y + 1) * CHUNK, :] = x * scale


def norm_kernel(piece_ref, unit_ref, scale_ref):
    x = piece_ref[...].reshape(WIDE, ROWS)
    scale = lax.rsqrt(jnp.sum(x * x, axis=0, keepdims=True) + 1e-06)
    scale_ref[...] = scale
    unit_ref[...] = (x * scale).T


def rows_kernel(own_ref, oth_ref, hi_ref, lo_ref):
    for j, ref in enumerate((own_ref, oth_ref)):
        at = slice(j * ROWS, (j + 1) * ROWS)
        hi_ref[at, :], lo_ref[at, :] = split(ref[...])


def tile_masks(pos_ref, half, part):
    zy, core, me = pos_ref[0], pos_ref[1], pos_ref[2]
    lane = lax.broadcasted_iota(jnp.int32, (1, NCOL), 1)
    col = ((lane // CHUNK) * NC + core) * ROWS + me * CHUNK + lane % CHUNK
    row = (zy * NC + half) * ROWS + lax.broadcasted_iota(jnp.int32, (ROWS, 1), 0)
    return col == row, col == part


def score_kernel(pos_ref, hi_ref, lo_ref, ownp_ref, othp_ref, far_ref, s_ref, row_ref, col_ref, cols_ref, sems):
    core = pos_ref[1]
    step = 256
    copies = []
    for i in range(NCOL // step):
        at = pl.ds(i * step, step)
        copies.append(pltpu.make_async_copy(far_ref.at[at, :], cols_ref.at[at, :], sems.at[i]))
        copies[-1].start()
    for i, copy in enumerate(copies):
        at = slice(i * step, (i + 1) * step)
        copy.wait()
        s_ref[:, at] = INV_TAU * dot3((hi_ref[...], lo_ref[...]), split(cols_ref[at, :]), ((1,), (1,)))
    colsum = jnp.zeros((1, NCOL), jnp.float32)
    pos = jnp.zeros((1, ROWS), jnp.float32)
    sums = []
    for j, part in enumerate((ownp_ref, othp_ref)):
        s = s_ref[j * ROWS:(j + 1) * ROWS, :]
        diag, hit = tile_masks(pos_ref, core ^ j, part[...])
        e = jnp.where(diag, 0.0, jnp.exp(s))
        colsum = colsum + jnp.sum(e, axis=0, keepdims=True)
        lanes = e[:, :ROWS]
        hits = jnp.sum(jnp.where(hit, s, 0.0), axis=0, keepdims=True)
        for c in range(NCOL // ROWS):
            pos = pos + hits[:, c * ROWS:(c + 1) * ROWS]
            if c:
                lanes = lanes + e[:, c * ROWS:(c + 1) * ROWS]
        sums.append(jnp.sum(lanes.T, axis=0, keepdims=True))
    first = core == 0
    row = jnp.concatenate([jnp.where(first, sums[0], sums[1]), jnp.where(first, sums[1], sums[0]),
                           jnp.zeros((8 - NC, ROWS), jnp.float32)], axis=0)
    nrow = NCOL // ROWS
    col = jnp.concatenate([colsum[:, c * ROWS:(c + 1) * ROWS] for c in range(nrow)]
                          + [pos, jnp.zeros((7 - nrow, ROWS), jnp.float32)], axis=0)
    for k in range(NC * NF):
        row_ref[k] = row
    for k in range(NZ * NYH):
        col_ref[k] = col


def grad_kernel(pos_ref, s_ref, cols_ref, ownp_ref, othp_ref, rows_ref, cols_l_ref, mine_ref, theirs_ref, w_hi, w_lo):
    core = pos_ref[1]
    row_l = jnp.sum(rows_ref[...], axis=0)
    col_l = jnp.sum(cols_l_ref[...], axis=0)
    nrow = NCOL // ROWS
    col_inv = jnp.concatenate([1.0 / col_l[c:c + 1, :] for c in range(nrow)], axis=1)
    loss = jnp.sum(jnp.log(col_l[:nrow, :]), axis=0, keepdims=True) - col_l[nrow:nrow + 1, :]
    projs = []
    for j, part in enumerate((ownp_ref, othp_ref)):
        s = s_ref[j * ROWS:(j + 1) * ROWS, :]
        half = core ^ j
        diag, hit = tile_masks(pos_ref, half, part[...])
        inv = column(1.0 / jnp.where(half == 0, row_l[0:1, :], row_l[1:2, :]))
        w = jnp.where(diag, 0.0, jnp.exp(s) * (inv + col_inv)) - jnp.where(hit, 2.0, 0.0)
        ws = w * s
        lanes = sum(ws[:, c * ROWS:(c + 1) * ROWS] for c in range(NCOL // ROWS))
        projs.append(jnp.sum(lanes.T, axis=0, keepdims=True))
        w_hi[j], w_lo[j] = split(w)
    weights = (w_hi[...].reshape(NC * ROWS, NCOL), w_lo[...].reshape(NC * ROWS, NCOL))
    step = 4 * FEAT
    tails = [jnp.concatenate([loss, proj, jnp.zeros((6, ROWS), jnp.float32)], axis=0) for proj in projs]
    for c in range(WIDE // step):
        at = slice(c * step, (c + 1) * step)
        g = INV_TAU * dot3(weights, split(cols_ref[:, at]), ((1,), (0,)))
        for j, out in enumerate((mine_ref, theirs_ref)):
            t = g[j * ROWS:(j + 1) * ROWS, :].T
            for p in range(4):
                out[4 * c + p, :FEAT, :] = t[p * FEAT:(p + 1) * FEAT, :]
                out[4 * c + p, FEAT:, :] = tails[j]


def last_kernel(piece_ref, scale_ref, view_ref, loss_ref, grad_ref):
    total = jnp.sum(piece_ref[...], axis=0)
    loss_ref[...] = jnp.sum(total[FEAT:FEAT + 1, :], axis=1, keepdims=True) / TOTAL
    scale = scale_ref[...]
    grad_ref[...] = (total[:FEAT, :] - view_ref[...] * scale * total[FEAT + 1:FEAT + 2, :]) * scale


def swap(x, axes, size, k):
    return lax.ppermute(x, axes, [(i, i ^ k) for i in range(size)])


def trade(x, axes):
    return lax.all_to_all(x, axes, 0, 0, tiled=True)


def call(body, name, outs, args, scratch=(), far=(), limit=24):
    return pl.pallas_call(
        body,
        out_shape=outs,
        in_specs=[SMEM if a.shape == (3,) else HBM if i in far else VMEM for i, a in enumerate(args)],
        out_specs=[VMEM] * len(outs),
        scratch_shapes=list(scratch),
        compiler_params=pltpu.CompilerParams(vmem_limit_bytes=limit * 1024 * 1024),
        name=name,
    )(*args)


def per_device(views, partner):
    zy = lax.axis_index(("z", "yh"))
    core = lax.axis_index("core")
    me = lax.axis_index(("yl", "x"))
    pos = jnp.stack([zy, core, me]).astype(jnp.int32)
    feat = ("yl", "x")

    packed = CHUNK * FEAT // ROWS
    chunks, copy = call(chunk_kernel, "chunks", [f32(NYH * NF, packed, ROWS), f32(FEAT, ROWS)], [views.T])
    chunk, copies = call(column_kernel, "columns", [f32(BLOCK, WIDE), f32(NF, FEAT, ROWS)],
                         [trade(chunks, ("yh", "yl", "x")), copy])
    far = lax.all_gather(chunk, "z", axis=0, tiled=True)
    own, scale = call(norm_kernel, "norm", [f32(ROWS, WIDE), f32(1, ROWS)], [trade(copies, feat)])
    hi, lo = call(rows_kernel, "rows", [jax.ShapeDtypeStruct((NC * ROWS, WIDE), jnp.bfloat16)] * 2,
                  [own, swap(own, "core", NC, 1)])
    own_p = partner.reshape(ROWS, 1)
    oth_p = swap(partner, "core", NC, 1).reshape(ROWS, 1)
    s, row, col, cols = call(
        score_kernel, "scores",
        [f32(NC * ROWS, NCOL), f32(NC * NF, 8, ROWS), f32(NZ * NYH, 8, ROWS), f32(NCOL, WIDE)],
        [pos, hi, lo, own_p, oth_p, far],
        [pltpu.SemaphoreType.DMA((NCOL // 256,))],
        far=(5,), limit=48,
    )
    rows_l = trade(row, ("core", "yl", "x"))
    cols_l = trade(col, ("z", "yh"))
    mine, theirs = call(
        grad_kernel, "gradient",
        [f32(NF, PIECE, ROWS)] * 2,
        [pos, s, cols, own_p, oth_p, rows_l, cols_l],
        [pltpu.VMEM((NC, ROWS, NCOL), jnp.bfloat16)] * 2,
    )
    pieces = trade(mine + swap(theirs, "core", NC, 1), feat)
    loss, grad = call(last_kernel, "finish", [f32(1, 1), f32(FEAT, ROWS)], [pieces, scale, copy])
    return loss.reshape(()), grad.T


def solution(mesh):
    fine = Mesh(mesh.devices.reshape(NZ, NYH, NC, NYL, NX), ("z", "yh", "core", "yl", "x"))
    rows = ("z", "yh", "core")
    return jax.shard_map(
        per_device,
        mesh=fine,
        in_specs=(P(rows, ("yl", "x")), P(rows)),
        out_specs=(P(), P(rows, ("yl", "x"))),
        check_vma=False,
    )
```

```python
import functools

import jax
import jax.numpy as jnp
from jax import lax
from jax.experimental import pallas as pl
from jax.experimental.pallas import tpu as pltpu
from jax.sharding import Mesh, PartitionSpec as P

NZ, NYH, NC, NYL, NX = 8, 4, 2, 2, 4
NF = NYL * NX
ROWS = 128
FEAT = 192
WIDE = NF * FEAT
CHUNK = ROWS // NF
NCOL = NZ * NYH * CHUNK
PIECE = FEAT + 8
BLOCK = NYH * CHUNK
TOTAL = 8192
INV_TAU = 10.0
VMEM = pl.BlockSpec(memory_space=pltpu.VMEM)
SMEM = pl.BlockSpec(memory_space=pltpu.SMEM)
HBM = pl.BlockSpec(memory_space=pltpu.HBM)


def f32(*shape):
    return jax.ShapeDtypeStruct(shape, jnp.float32)


def split(x):
    hi = x.astype(jnp.bfloat16)
    lo = (x - hi.astype(jnp.float32)).astype(jnp.bfloat16)
    return hi, lo


def dot3(a, b, dims):
    def one(x, y):
        return lax.dot_general(x, y, (dims, ((), ())), preferred_element_type=jnp.float32)
    return one(a[0], b[0]) + (one(a[0], b[1]) + one(a[1], b[0]))


def column(x):
    return jnp.broadcast_to(x, (ROWS, ROWS)).T[:, :1]


def pack(x):
    half = CHUNK // 2
    return jnp.concatenate([x[:, :ROWS], jnp.concatenate([x[:half, ROWS:], x[half:, ROWS:]], axis=1)], axis=0)


def unpack(x):
    tail = x[CHUNK:, :]
    rest = FEAT - ROWS
    return jnp.concatenate([x[:CHUNK, :], jnp.concatenate([tail[:, :rest], tail[:, rest:]], axis=0)], axis=1)


def chunk_kernel(view_ref, out_ref, copy_ref):
    copy_ref[...] = view_ref[...]
    x = view_ref[...].T
    for f in range(NF):
        piece = pack(x[f * CHUNK:(f + 1) * CHUNK, :])
        for y in range(NYH):
            out_ref[y * NF + f] = piece


def copies_kernel(view_ref, after_ref, copies_ref):
    for f in range(NF):
        copies_ref[f] = view_ref[...]


def column_kernel(piece_ref, unit_ref):
    for y in range(NYH):
        x = jnp.concatenate([unpack(piece_ref[y * NF + f]) for f in range(NF)], axis=1)
        scale = lax.rsqrt(jnp.sum(x * x, axis=1, keepdims=True) + 1e-06)
        unit_ref[y * CHUNK:(y + 1) * CHUNK, :] = x * scale


def norm_kernel(piece_ref, unit_ref, scale_ref):
    x = piece_ref[...].reshape(WIDE, ROWS)
    scale = lax.rsqrt(jnp.sum(x * x, axis=0, keepdims=True) + 1e-06)
    scale_ref[...] = scale
    unit_ref[...] = (x * scale).T


def rows_kernel(own_ref, oth_ref, hi_ref, lo_ref):
    for j, ref in enumerate((own_ref, oth_ref)):
        at = slice(j * ROWS, (j + 1) * ROWS)
        hi_ref[at, :], lo_ref[at, :] = split(ref[...])


def tile_masks(pos_ref, half, part):
    zy, core, me = pos_ref[0], pos_ref[1], pos_ref[2]
    lane = lax.broadcasted_iota(jnp.int32, (1, NCOL), 1)
    col = ((lane // CHUNK) * NC + core) * ROWS + me * CHUNK + lane % CHUNK
    row = (zy * NC + half) * ROWS + lax.broadcasted_iota(jnp.int32, (ROWS, 1), 0)
    return col == row, col == part


def score_kernel(pos_ref, hi_ref, lo_ref, ownp_ref, othp_ref, far_ref, s_ref, row_ref, col_ref, cols_ref, sems):
    core = pos_ref[1]
    step = 256
    copies = []
    for i in range(NCOL // step):
        at = pl.ds(i * step, step)
        copies.append(pltpu.make_async_copy(far_ref.at[at, :], cols_ref.at[at, :], sems.at[i]))
        copies[-1].start()
    for i, copy in enumerate(copies):
        at = slice(i * step, (i + 1) * step)
        copy.wait()
        s_ref[:, at] = INV_TAU * dot3((hi_ref[...], lo_ref[...]), split(cols_ref[at, :]), ((1,), (1,)))
    colsum = jnp.zeros((1, NCOL), jnp.float32)
    pos = jnp.zeros((1, ROWS), jnp.float32)
    sums = []
    for j, part in enumerate((ownp_ref, othp_ref)):
        s = s_ref[j * ROWS:(j + 1) * ROWS, :]
        diag, hit = tile_masks(pos_ref, core ^ j, part[...])
        e = jnp.where(diag, 0.0, jnp.exp(s))
        colsum = colsum + jnp.sum(e, axis=0, keepdims=True)
        lanes = e[:, :ROWS]
        hits = jnp.sum(jnp.where(hit, s, 0.0), axis=0, keepdims=True)
        for c in range(NCOL // ROWS):
            pos = pos + hits[:, c * ROWS:(c + 1) * ROWS]
            if c:
                lanes = lanes + e[:, c * ROWS:(c + 1) * ROWS]
        sums.append(jnp.sum(lanes.T, axis=0, keepdims=True))
    first = core == 0
    row = jnp.concatenate([jnp.where(first, sums[0], sums[1]), jnp.where(first, sums[1], sums[0]),
                           jnp.zeros((8 - NC, ROWS), jnp.float32)], axis=0)
    nrow = NCOL // ROWS
    col = jnp.concatenate([colsum[:, c * ROWS:(c + 1) * ROWS] for c in range(nrow)]
                          + [pos, jnp.zeros((7 - nrow, ROWS), jnp.float32)], axis=0)
    for k in range(NC * NF):
        row_ref[k] = row
    for k in range(NZ * NYH):
        col_ref[k] = col


def grad_kernel(j, pos_ref, s_ref, cols_ref, part_ref, rows_ref, cols_l_ref, out_ref):
    core = pos_ref[1]
    row_l = jnp.sum(rows_ref[...], axis=0)
    col_l = jnp.sum(cols_l_ref[...], axis=0)
    nrow = NCOL // ROWS
    col_inv = jnp.concatenate([1.0 / col_l[c:c + 1, :] for c in range(nrow)], axis=1)
    loss = jnp.sum(jnp.log(col_l[:nrow, :]), axis=0, keepdims=True) - col_l[nrow:nrow + 1, :]
    s = s_ref[j * ROWS:(j + 1) * ROWS, :]
    half = core ^ j
    diag, hit = tile_masks(pos_ref, half, part_ref[...])
    inv = column(1.0 / jnp.where(half == 0, row_l[0:1, :], row_l[1:2, :]))
    w = jnp.where(diag, 0.0, jnp.exp(s) * (inv + col_inv)) - jnp.where(hit, 2.0, 0.0)
    ws = w * s
    lanes = sum(ws[:, c * ROWS:(c + 1) * ROWS] for c in range(NCOL // ROWS))
    proj = jnp.sum(lanes.T, axis=0, keepdims=True)
    weights = split(w)
    step = 4 * FEAT
    tail = jnp.concatenate([loss, proj, jnp.zeros((6, ROWS), jnp.float32)], axis=0)
    for c in range(WIDE // step):
        at = slice(c * step, (c + 1) * step)
        t = (INV_TAU * dot3(weights, split(cols_ref[:, at]), ((1,), (0,)))).T
        for p in range(4):
            out_ref[4 * c + p, :FEAT, :] = t[p * FEAT:(p + 1) * FEAT, :]
            out_ref[4 * c + p, FEAT:, :] = tail


def last_kernel(piece_ref, scale_ref, view_ref, loss_ref, grad_ref):
    total = jnp.sum(piece_ref[...], axis=0)
    loss_ref[...] = jnp.sum(total[FEAT:FEAT + 1, :], axis=1, keepdims=True) / TOTAL
    scale = scale_ref[...]
    grad_ref[...] = (total[:FEAT, :] - view_ref[...] * scale * total[FEAT + 1:FEAT + 2, :]) * scale


def swap(x, axes, size, k):
    return lax.ppermute(x, axes, [(i, i ^ k) for i in range(size)])


def trade(x, axes):
    return lax.all_to_all(x, axes, 0, 0, tiled=True)


def call(body, name, outs, args, scratch=(), far=(), limit=24):
    return pl.pallas_call(
        body,
        out_shape=outs,
        in_specs=[SMEM if a.shape == (3,) else HBM if i in far else VMEM for i, a in enumerate(args)],
        out_specs=[VMEM] * len(outs),
        scratch_shapes=list(scratch),
        compiler_params=pltpu.CompilerParams(vmem_limit_bytes=limit * 1024 * 1024),
        name=name,
    )(*args)


def per_device(views, partner):
    zy = lax.axis_index(("z", "yh"))
    core = lax.axis_index("core")
    me = lax.axis_index(("yl", "x"))
    pos = jnp.stack([zy, core, me]).astype(jnp.int32)
    feat = ("yl", "x")

    packed = CHUNK * FEAT // ROWS
    chunks, copy = call(chunk_kernel, "chunks", [f32(NYH * NF, packed, ROWS), f32(FEAT, ROWS)], [views.T])
    chunk, = call(column_kernel, "columns", [f32(BLOCK, WIDE)], [trade(chunks, ("yh", "yl", "x"))])
    far = lax.all_gather(chunk, "z", axis=0, tiled=True)
    copies, = call(copies_kernel, "copies", [f32(NF, FEAT, ROWS)], [copy, chunk], far=(1,))
    own, scale = call(norm_kernel, "norm", [f32(ROWS, WIDE), f32(1, ROWS)], [trade(copies, feat)])
    hi, lo = call(rows_kernel, "rows", [jax.ShapeDtypeStruct((NC * ROWS, WIDE), jnp.bfloat16)] * 2,
                  [own, swap(own, "core", NC, 1)])
    own_p = partner.reshape(ROWS, 1)
    oth_p = swap(partner, "core", NC, 1).reshape(ROWS, 1)
    s, row, col, cols = call(
        score_kernel, "scores",
        [f32(NC * ROWS, NCOL), f32(NC * NF, 8, ROWS), f32(NZ * NYH, 8, ROWS), f32(NCOL, WIDE)],
        [pos, hi, lo, own_p, oth_p, far],
        [pltpu.SemaphoreType.DMA((NCOL // 256,))],
        far=(5,), limit=48,
    )
    rows_l = trade(row, ("core", "yl", "x"))
    cols_l = trade(col, ("z", "yh"))
    theirs, mine = (
        call(functools.partial(grad_kernel, j), name, [f32(NF, PIECE, ROWS)], [pos, s, cols, part, rows_l, cols_l])[0]
        for j, name, part in ((1, "theirs", oth_p), (0, "mine", own_p))
    )
    pieces = trade(mine + swap(theirs, "core", NC, 1), feat)
    loss, grad = call(last_kernel, "finish", [f32(1, 1), f32(FEAT, ROWS)], [pieces, scale, copy])
    return loss.reshape(()), grad.T


def solution(mesh):
    fine = Mesh(mesh.devices.reshape(NZ, NYH, NC, NYL, NX), ("z", "yh", "core", "yl", "x"))
    rows = ("z", "yh", "core")
    return jax.shard_map(
        per_device,
        mesh=fine,
        in_specs=(P(rows, ("yl", "x")), P(rows)),
        out_specs=(P(), P(rows, ("yl", "x"))),
        check_vma=False,
    )
```

```python
import functools

import jax
import jax.numpy as jnp
from jax import lax
from jax.experimental import pallas as pl
from jax.experimental.pallas import tpu as pltpu
from jax.sharding import Mesh, PartitionSpec as P

NZ, NYH, NC, NYL, NX = 8, 4, 2, 2, 4
NF = NYL * NX
ROWS = 128
FEAT = 192
WIDE = NF * FEAT
CHUNK = ROWS // NF
NCOL = NZ * NYH * CHUNK
PIECE = FEAT + 8
BLOCK = NYH * CHUNK
HALF = BLOCK // 2
TOTAL = 8192
INV_TAU = 10.0
VMEM = pl.BlockSpec(memory_space=pltpu.VMEM)
SMEM = pl.BlockSpec(memory_space=pltpu.SMEM)
PARAMS = pltpu.CompilerParams(vmem_limit_bytes=32 * 1024 * 1024)


def f32(*shape):
    return jax.ShapeDtypeStruct(shape, jnp.float32)


def split(x):
    hi = x.astype(jnp.bfloat16)
    lo = (x - hi.astype(jnp.float32)).astype(jnp.bfloat16)
    return hi, lo


def dot3(a, b, dims):
    def one(x, y):
        return lax.dot_general(x, y, (dims, ((), ())), preferred_element_type=jnp.float32)
    return one(a[0], b[0]) + (one(a[0], b[1]) + one(a[1], b[0]))


def column(x):
    return jnp.broadcast_to(x, (ROWS, ROWS)).T[:, :1]


def pack(x):
    half = CHUNK // 2
    return jnp.concatenate([x[:, :ROWS], jnp.concatenate([x[:half, ROWS:], x[half:, ROWS:]], axis=1)], axis=0)


def unpack(x):
    tail = x[CHUNK:, :]
    rest = FEAT - ROWS
    return jnp.concatenate([x[:CHUNK, :], jnp.concatenate([tail[:, :rest], tail[:, rest:]], axis=0)], axis=1)


def chunk_kernel(view_ref, out_ref, copy_ref):
    copy_ref[...] = view_ref[...]
    x = view_ref[...].T
    for f in range(NF):
        piece = pack(x[f * CHUNK:(f + 1) * CHUNK, :])
        for y in range(NYH):
            out_ref[y * NF + f] = piece


def column_kernel(piece_ref, view_ref, partner_ref, unit_ref, shard_ref):
    shard_ref[:FEAT, :] = view_ref[...]
    shard_ref[FEAT:, :] = jnp.broadcast_to(partner_ref[...].astype(jnp.float32), (PIECE - FEAT, ROWS))
    for y in range(NYH):
        x = jnp.concatenate([unpack(piece_ref[y * NF + f]) for f in range(NF)], axis=1)
        scale = lax.rsqrt(jnp.sum(x * x, axis=1, keepdims=True) + 1e-06)
        unit_ref[y * CHUNK:(y + 1) * CHUNK, :] = x * scale


def norm_kernel(pos_ref, piece_ref, scale_ref, ownp_ref, othp_ref, hi_ref, lo_ref):
    core = pos_ref[1]
    for j, part in enumerate((ownp_ref, othp_ref)):
        x = piece_ref[core ^ j, :, :FEAT, :].reshape(WIDE, ROWS)
        scale = lax.rsqrt(jnp.sum(x * x, axis=0, keepdims=True) + 1e-06)
        if j == 0:
            scale_ref[...] = scale
        units = (x * scale).T
        part[...] = column(piece_ref[core ^ j, 0, FEAT:FEAT + 1, :]).astype(jnp.int32)
        at = slice(j * ROWS, (j + 1) * ROWS)
        hi_ref[at, :], lo_ref[at, :] = split(units)


def tile_masks(pos_ref, half, part):
    zy, core, me = pos_ref[0], pos_ref[1], pos_ref[2]
    lane = lax.broadcasted_iota(jnp.int32, (1, NCOL), 1)
    col = ((lane // CHUNK) * NC + core) * ROWS + me * CHUNK + lane % CHUNK
    row = (zy * NC + half) * ROWS + lax.broadcasted_iota(jnp.int32, (ROWS, 1), 0)
    return col == row, col == part


def place(z, ahead):
    return (z + NZ + ahead * (1 - 2 * (z % 2))) % NZ * BLOCK


def gather_blocks(z, blocks, cols_ref):
    for k, block in enumerate(blocks):
        ahead = k if k < NZ // 2 else NZ // 2 - 1 - k
        cols_ref[pl.ds(pl.multiple_of(place(z, ahead), BLOCK), BLOCK), :] = block[...]


def early_kernel(pos_ref, hi_ref, lo_ref, *refs):
    blocks, (s_ref, cols) = refs[:-2], refs[-2:]
    z = pos_ref[0] // NYH
    gather_blocks(z, blocks, cols)
    late = pl.multiple_of(place(z, NZ // 2), BLOCK)
    cols[pl.ds(late, BLOCK), :] = jnp.zeros((BLOCK, WIDE), jnp.float32)
    rows = (hi_ref[...], lo_ref[...])
    step = 256
    for c in range(0, NCOL, step):
        s_ref[:, c:c + step] = INV_TAU * dot3(rows, split(cols[c:c + step, :]), ((1,), (1,)))


def score_kernel(pos_ref, hi_ref, lo_ref, ownp_ref, othp_ref, early_ref, *refs):
    blocks, (s_ref, row_ref, col_ref, cols_ref) = refs[:-4], refs[-4:]
    core = pos_ref[1]
    z = pos_ref[0] // NYH
    gather_blocks(z, blocks[:-2], cols_ref)
    late = place(z, NZ // 2)
    for k, half in enumerate(blocks[-2:]):
        cols_ref[pl.ds(pl.multiple_of(late + k * HALF, HALF), HALF), :] = half[...]
    s_ref[...] = early_ref[...]
    at = pl.ds(pl.multiple_of(late // ROWS * ROWS, ROWS), ROWS)
    s_ref[:, at] = INV_TAU * dot3((hi_ref[...], lo_ref[...]), split(cols_ref[at, :]), ((1,), (1,)))
    colsum = jnp.zeros((1, NCOL), jnp.float32)
    pos = jnp.zeros((1, ROWS), jnp.float32)
    sums = []
    for j, part in enumerate((ownp_ref, othp_ref)):
        s = s_ref[j * ROWS:(j + 1) * ROWS, :]
        diag, hit = tile_masks(pos_ref, core ^ j, part[...])
        e = jnp.where(diag, 0.0, jnp.exp(s))
        colsum = colsum + jnp.sum(e, axis=0, keepdims=True)
        lanes = e[:, :ROWS]
        hits = jnp.sum(jnp.where(hit, s, 0.0), axis=0, keepdims=True)
        for c in range(NCOL // ROWS):
            pos = pos + hits[:, c * ROWS:(c + 1) * ROWS]
            if c:
                lanes = lanes + e[:, c * ROWS:(c + 1) * ROWS]
        sums.append(jnp.sum(lanes.T, axis=0, keepdims=True))
    first = core == 0
    row = jnp.concatenate([jnp.where(first, sums[0], sums[1]), jnp.where(first, sums[1], sums[0]),
                           jnp.zeros((8 - NC, ROWS), jnp.float32)], axis=0)
    nrow = NCOL // ROWS
    col = jnp.concatenate([colsum[:, c * ROWS:(c + 1) * ROWS] for c in range(nrow)]
                          + [pos, jnp.zeros((7 - nrow, ROWS), jnp.float32)], axis=0)
    for k in range(NC * NF):
        row_ref[k] = row
    for k in range(NZ * NYH):
        col_ref[k] = col


def grad_kernel(j, pos_ref, s_ref, cols_ref, part_ref, rows_ref, cols_l_ref, out_ref):
    core = pos_ref[1]
    row_l = jnp.sum(rows_ref[...], axis=0)
    col_l = jnp.sum(cols_l_ref[...], axis=0)
    nrow = NCOL // ROWS
    col_inv = jnp.concatenate([1.0 / col_l[c:c + 1, :] for c in range(nrow)], axis=1)
    loss = jnp.sum(jnp.log(col_l[:nrow, :]), axis=0, keepdims=True) - col_l[nrow:nrow + 1, :]
    s = s_ref[j * ROWS:(j + 1) * ROWS, :]
    half = core ^ j
    diag, hit = tile_masks(pos_ref, half, part_ref[...])
    inv = column(1.0 / jnp.where(half == 0, row_l[0:1, :], row_l[1:2, :]))
    w = jnp.where(diag, 0.0, jnp.exp(s) * (inv + col_inv)) - jnp.where(hit, 2.0, 0.0)
    ws = w * s
    lanes = sum(ws[:, c * ROWS:(c + 1) * ROWS] for c in range(NCOL // ROWS))
    proj = jnp.sum(lanes.T, axis=0, keepdims=True)
    weights = split(w)
    step = 4 * FEAT
    tail = jnp.concatenate([loss, proj, jnp.zeros((6, ROWS), jnp.float32)], axis=0)
    for c in range(WIDE // step):
        at = slice(c * step, (c + 1) * step)
        t = (INV_TAU * dot3(weights, split(cols_ref[:, at]), ((1,), (0,)))).T
        for p in range(4):
            out_ref[4 * c + p, :FEAT, :] = t[p * FEAT:(p + 1) * FEAT, :]
            out_ref[4 * c + p, FEAT:, :] = tail


def last_kernel(piece_ref, scale_ref, view_ref, loss_ref, grad_ref):
    total = jnp.sum(piece_ref[...], axis=0)
    loss_ref[...] = jnp.sum(total[FEAT:FEAT + 1, :], axis=1, keepdims=True) / TOTAL
    scale = scale_ref[...]
    grad_ref[...] = (total[:FEAT, :] - view_ref[...] * scale * total[FEAT + 1:FEAT + 2, :]) * scale


def swap(x, axes, size, k):
    return lax.ppermute(x, axes, [(i, i ^ k) for i in range(size)])


def around(x):
    pair = [(i, i ^ 1) for i in range(NZ)]
    between = [(i, ((i - 1) ^ 1) + 1 & NZ - 1) for i in range(NZ)]
    a, b = [x], [x]
    for _ in range(NZ // 2 - 1):
        got = lax.ppermute(b[-1], "z", pair), lax.ppermute(a[-1], "z", between)
        a.append(got[0])
        b.append(got[1])
    last = lax.ppermute(b[-1][:HALF], "z", pair), lax.ppermute(a[-1][HALF:], "z", between)
    return a + b[1:] + list(last)


def trade(x, axes):
    return lax.all_to_all(x, axes, 0, 0, tiled=True)


def call(body, name, outs, args, scratch=()):
    return pl.pallas_call(
        body,
        out_shape=outs,
        in_specs=[SMEM if a.shape == (3,) else VMEM for a in args],
        out_specs=[VMEM] * len(outs),
        scratch_shapes=list(scratch),
        compiler_params=PARAMS,
        name=name,
    )(*args)


def per_device(views, partner):
    zy = lax.axis_index(("z", "yh"))
    core = lax.axis_index("core")
    me = lax.axis_index(("yl", "x"))
    pos = jnp.stack([zy, core, me]).astype(jnp.int32)
    feat = ("yl", "x")

    packed = CHUNK * FEAT // ROWS
    chunks, copy = call(chunk_kernel, "chunks", [f32(NYH * NF, packed, ROWS), f32(FEAT, ROWS)], [views.T])
    chunk, shard = call(column_kernel, "columns", [f32(BLOCK, WIDE), f32(PIECE, ROWS)],
                        [trade(chunks, ("yh", "yl", "x")), copy, partner.reshape(1, ROWS)])
    whole = lax.all_gather(shard, ("core", "yl", "x"), axis=0, tiled=True)
    ring = around(chunk)
    ids, bf16 = jax.ShapeDtypeStruct((ROWS, 1), jnp.int32), jax.ShapeDtypeStruct((NC * ROWS, WIDE), jnp.bfloat16)
    scale, own_p, oth_p, hi, lo = call(
        norm_kernel, "norm",
        [f32(1, ROWS), ids, ids, bf16, bf16],
        [pos, whole.reshape(NC, NF, PIECE, ROWS)],
    )
    early, = call(early_kernel, "early", [f32(NC * ROWS, NCOL)], [pos, hi, lo, *ring[:-2]],
                  [pltpu.VMEM((NCOL, WIDE), jnp.float32)])
    s, row, col, cols = call(
        score_kernel, "scores",
        [f32(NC * ROWS, NCOL), f32(NC * NF, 8, ROWS), f32(NZ * NYH, 8, ROWS), f32(NCOL, WIDE)],
        [pos, hi, lo, own_p, oth_p, early, *ring],
    )
    rows_l = trade(row, ("core", "yl", "x"))
    cols_l = trade(col, ("z", "yh"))
    theirs, mine = (
        call(functools.partial(grad_kernel, j), name, [f32(NF, PIECE, ROWS)], [pos, s, cols, part, rows_l, cols_l])[0]
        for j, name, part in ((1, "theirs", oth_p), (0, "mine", own_p))
    )
    pieces = trade(mine + swap(theirs, "core", NC, 1), feat)
    loss, grad = call(last_kernel, "finish", [f32(1, 1), f32(FEAT, ROWS)], [pieces, scale, copy])
    return loss.reshape(()), grad.T


def solution(mesh):
    fine = Mesh(mesh.devices.reshape(NZ, NYH, NC, NYL, NX), ("z", "yh", "core", "yl", "x"))
    rows = ("z", "yh", "core")
    return jax.shard_map(
        per_device,
        mesh=fine,
        in_specs=(P(rows, ("yl", "x")), P(rows)),
        out_specs=(P(), P(rows, ("yl", "x"))),
        check_vma=False,
    )
```

```python
import functools

import jax
import jax.numpy as jnp
from jax import lax
from jax.experimental import pallas as pl
from jax.experimental.pallas import tpu as pltpu
from jax.sharding import Mesh, PartitionSpec as P

NZ, NYH, NC, NYL, NX = 8, 4, 2, 2, 4
NF = NYL * NX
ROWS = 128
FEAT = 192
WIDE = NF * FEAT
CHUNK = ROWS // NF
NCOL = NZ * NYH * CHUNK
PIECE = FEAT + 8
BLOCK = NYH * CHUNK
TOTAL = 8192
INV_TAU = 10.0
VMEM = pl.BlockSpec(memory_space=pltpu.VMEM)
SMEM = pl.BlockSpec(memory_space=pltpu.SMEM)
HBM = pl.BlockSpec(memory_space=pltpu.HBM)


def f32(*shape):
    return jax.ShapeDtypeStruct(shape, jnp.float32)


def split(x):
    hi = x.astype(jnp.bfloat16)
    lo = (x - hi.astype(jnp.float32)).astype(jnp.bfloat16)
    return hi, lo


def dot3(a, b, dims):
    def one(x, y):
        return lax.dot_general(x, y, (dims, ((), ())), preferred_element_type=jnp.float32)
    return one(a[0], b[0]) + (one(a[0], b[1]) + one(a[1], b[0]))


def column(x):
    return jnp.broadcast_to(x, (ROWS, ROWS)).T[:, :1]


def pack(x):
    half = CHUNK // 2
    return jnp.concatenate([x[:, :ROWS], jnp.concatenate([x[:half, ROWS:], x[half:, ROWS:]], axis=1)], axis=0)


def unpack(x):
    tail = x[CHUNK:, :]
    rest = FEAT - ROWS
    return jnp.concatenate([x[:CHUNK, :], jnp.concatenate([tail[:, :rest], tail[:, rest:]], axis=0)], axis=1)


def chunk_kernel(view_ref, out_ref, copy_ref):
    copy_ref[...] = view_ref[...]
    x = view_ref[...].T
    for f in range(NF):
        piece = pack(x[f * CHUNK:(f + 1) * CHUNK, :])
        for y in range(NYH):
            out_ref[y * NF + f] = piece


def copies_kernel(view_ref, after_ref, copies_ref):
    for f in range(NF):
        copies_ref[f] = view_ref[...]


def column_kernel(piece_ref, unit_ref):
    for y in range(NYH):
        x = jnp.concatenate([unpack(piece_ref[y * NF + f]) for f in range(NF)], axis=1)
        scale = lax.rsqrt(jnp.sum(x * x, axis=1, keepdims=True) + 1e-06)
        unit_ref[y * CHUNK:(y + 1) * CHUNK, :] = x * scale


def norm_kernel(piece_ref, unit_ref, scale_ref):
    x = piece_ref[...].reshape(WIDE, ROWS)
    scale = lax.rsqrt(jnp.sum(x * x, axis=0, keepdims=True) + 1e-06)
    scale_ref[...] = scale
    unit_ref[...] = (x * scale).T


def rows_kernel(own_ref, oth_ref, hi_ref, lo_ref):
    for j, ref in enumerate((own_ref, oth_ref)):
        at = slice(j * ROWS, (j + 1) * ROWS)
        hi_ref[at, :], lo_ref[at, :] = split(ref[...])


def tile_masks(pos_ref, half, part):
    zy, core, me = pos_ref[0], pos_ref[1], pos_ref[2]
    lane = lax.broadcasted_iota(jnp.int32, (1, NCOL), 1)
    col = ((lane // CHUNK) * NC + core) * ROWS + me * CHUNK + lane % CHUNK
    row = (zy * NC + half) * ROWS + lax.broadcasted_iota(jnp.int32, (ROWS, 1), 0)
    return col == row, col == part


def score_kernel(pos_ref, hi_ref, lo_ref, ownp_ref, othp_ref, far_ref, s_ref, row_ref, col_ref, cols_ref, sems):
    core = pos_ref[1]
    step = 128
    copies = []
    for i in range(NCOL // step):
        at = pl.ds(i * step, step)
        copies.append(pltpu.make_async_copy(far_ref.at[at, :], cols_ref.at[at, :], sems.at[i]))
        copies[-1].start()
    for i, copy in enumerate(copies):
        at = slice(i * step, (i + 1) * step)
        copy.wait()
        s_ref[:, at] = INV_TAU * dot3((hi_ref[...], lo_ref[...]), split(cols_ref[at, :]), ((1,), (1,)))
    colsum = jnp.zeros((1, NCOL), jnp.float32)
    pos = jnp.zeros((1, ROWS), jnp.float32)
    sums = []
    for j, part in enumerate((ownp_ref, othp_ref)):
        s = s_ref[j * ROWS:(j + 1) * ROWS, :]
        diag, hit = tile_masks(pos_ref, core ^ j, part[...])
        e = jnp.where(diag, 0.0, jnp.exp(s))
        colsum = colsum + jnp.sum(e, axis=0, keepdims=True)
        lanes = e[:, :ROWS]
        hits = jnp.sum(jnp.where(hit, s, 0.0), axis=0, keepdims=True)
        for c in range(NCOL // ROWS):
            pos = pos + hits[:, c * ROWS:(c + 1) * ROWS]
            if c:
                lanes = lanes + e[:, c * ROWS:(c + 1) * ROWS]
        sums.append(jnp.sum(lanes.T, axis=0, keepdims=True))
    first = core == 0
    row = jnp.concatenate([jnp.where(first, sums[0], sums[1]), jnp.where(first, sums[1], sums[0]),
                           jnp.zeros((8 - NC, ROWS), jnp.float32)], axis=0)
    nrow = NCOL // ROWS
    col = jnp.concatenate([colsum[:, c * ROWS:(c + 1) * ROWS] for c in range(nrow)]
                          + [pos, jnp.zeros((7 - nrow, ROWS), jnp.float32)], axis=0)
    for k in range(NC * NF):
        row_ref[k] = row
    for k in range(NZ * NYH):
        col_ref[k] = col


def grad_kernel(j, pos_ref, s_ref, cols_ref, part_ref, rows_ref, cols_l_ref, out_ref):
    core = pos_ref[1]
    row_l = jnp.sum(rows_ref[...], axis=0)
    col_l = jnp.sum(cols_l_ref[...], axis=0)
    nrow = NCOL // ROWS
    col_inv = jnp.concatenate([1.0 / col_l[c:c + 1, :] for c in range(nrow)], axis=1)
    loss = jnp.sum(jnp.log(col_l[:nrow, :]), axis=0, keepdims=True) - col_l[nrow:nrow + 1, :]
    s = s_ref[j * ROWS:(j + 1) * ROWS, :]
    half = core ^ j
    diag, hit = tile_masks(pos_ref, half, part_ref[...])
    inv = column(1.0 / jnp.where(half == 0, row_l[0:1, :], row_l[1:2, :]))
    w = jnp.where(diag, 0.0, jnp.exp(s) * (inv + col_inv)) - jnp.where(hit, 2.0, 0.0)
    ws = w * s
    lanes = sum(ws[:, c * ROWS:(c + 1) * ROWS] for c in range(NCOL // ROWS))
    proj = jnp.sum(lanes.T, axis=0, keepdims=True)
    weights = split(w)
    step = 4 * FEAT
    tail = jnp.concatenate([loss, proj, jnp.zeros((6, ROWS), jnp.float32)], axis=0)
    for c in range(WIDE // step):
        at = slice(c * step, (c + 1) * step)
        t = (INV_TAU * dot3(weights, split(cols_ref[:, at]), ((1,), (0,)))).T
        for p in range(4):
            out_ref[4 * c + p, :FEAT, :] = t[p * FEAT:(p + 1) * FEAT, :]
            out_ref[4 * c + p, FEAT:, :] = tail


def last_kernel(piece_ref, scale_ref, view_ref, loss_ref, grad_ref):
    total = jnp.sum(piece_ref[...], axis=0)
    loss_ref[...] = jnp.sum(total[FEAT:FEAT + 1, :], axis=1, keepdims=True) / TOTAL
    scale = scale_ref[...]
    grad_ref[...] = (total[:FEAT, :] - view_ref[...] * scale * total[FEAT + 1:FEAT + 2, :]) * scale


def swap(x, axes, size, k):
    return lax.ppermute(x, axes, [(i, i ^ k) for i in range(size)])


def trade(x, axes):
    return lax.all_to_all(x, axes, 0, 0, tiled=True)


def call(body, name, outs, args, scratch=(), far=(), limit=24):
    return pl.pallas_call(
        body,
        out_shape=outs,
        in_specs=[SMEM if a.shape == (3,) else HBM if i in far else VMEM for i, a in enumerate(args)],
        out_specs=[VMEM] * len(outs),
        scratch_shapes=list(scratch),
        compiler_params=pltpu.CompilerParams(vmem_limit_bytes=limit * 1024 * 1024),
        name=name,
    )(*args)


def per_device(views, partner):
    zy = lax.axis_index(("z", "yh"))
    core = lax.axis_index("core")
    me = lax.axis_index(("yl", "x"))
    pos = jnp.stack([zy, core, me]).astype(jnp.int32)
    feat = ("yl", "x")

    packed = CHUNK * FEAT // ROWS
    chunks, copy = call(chunk_kernel, "chunks", [f32(NYH * NF, packed, ROWS), f32(FEAT, ROWS)], [views.T])
    chunk, = call(column_kernel, "columns", [f32(BLOCK, WIDE)], [trade(chunks, ("yh", "yl", "x"))])
    far = lax.all_gather(chunk, "z", axis=0, tiled=True)
    copies, = call(copies_kernel, "copies", [f32(NF, FEAT, ROWS)], [copy, chunk], far=(1,))
    own, scale = call(norm_kernel, "norm", [f32(ROWS, WIDE), f32(1, ROWS)], [trade(copies, feat)])
    hi, lo = call(rows_kernel, "rows", [jax.ShapeDtypeStruct((NC * ROWS, WIDE), jnp.bfloat16)] * 2,
                  [own, swap(own, "core", NC, 1)])
    own_p = partner.reshape(ROWS, 1)
    oth_p = swap(partner, "core", NC, 1).reshape(ROWS, 1)
    s, row, col, cols = call(
        score_kernel, "scores",
        [f32(NC * ROWS, NCOL), f32(NC * NF, 8, ROWS), f32(NZ * NYH, 8, ROWS), f32(NCOL, WIDE)],
        [pos, hi, lo, own_p, oth_p, far],
        [pltpu.SemaphoreType.DMA((NCOL // 128,))],
        far=(5,), limit=48,
    )
    rows_l = trade(row, ("core", "yl", "x"))
    cols_l = trade(col, ("z", "yh"))
    theirs, mine = (
        call(functools.partial(grad_kernel, j), name, [f32(NF, PIECE, ROWS)], [pos, s, cols, part, rows_l, cols_l])[0]
        for j, name, part in ((1, "theirs", oth_p), (0, "mine", own_p))
    )
    pieces = trade(mine + swap(theirs, "core", NC, 1), feat)
    loss, grad = call(last_kernel, "finish", [f32(1, 1), f32(FEAT, ROWS)], [pieces, scale, copy])
    return loss.reshape(()), grad.T


def solution(mesh):
    fine = Mesh(mesh.devices.reshape(NZ, NYH, NC, NYL, NX), ("z", "yh", "core", "yl", "x"))
    rows = ("z", "yh", "core")
    return jax.shard_map(
        per_device,
        mesh=fine,
        in_specs=(P(rows, ("yl", "x")), P(rows)),
        out_specs=(P(), P(rows, ("yl", "x"))),
        check_vma=False,
    )
```
